512 devices in a mesh: seq: 32 (over y, x), et: 16 (over z, core).
Axes of the slice: x: 4, y: 8, z: 8, core: 2. Of those that a mesh axis runs over, the one named last changes fastest.
Arguments:
- z_in: bfloat16 [8192, 2048], P('seq', 'et'), may hold values from -6 to 6
- out_grad: bfloat16 [8192, 2048], P('seq', 'et'), may hold values from -6 to 6
- gates: float32 [8192, 2], P('seq'), may hold values from 0.2 to 1
- expert_ids: int32 [8192, 2], P('seq'), may hold values from 0 to 31, all different within a row; in each aligned block of 256 rows (0 to 255, 256 to 511, ...) at most 24 rows name the same one
- w_gate: bfloat16 [32, 2048, 5632], P('seq', None, 'et'), may hold values from -0.125 to 0.125
- w_up: bfloat16 [32, 2048, 5632], P('seq', None, 'et'), may hold values from -0.125 to 0.125
- w_down: bfloat16 [32, 5632, 2048], P('seq', 'et'), may hold values from -0.078125 to 0.078125
- queries: bfloat16 [8192, 2048], P('seq', 'et'), may hold values from -48 to 48
- keys: bfloat16 [8192, 2048], P('seq', 'et'), may hold values from -18 to 18
- values: bfloat16 [8192, 2048], P('seq', 'et'), may hold values from -6 to 6
- band_bounds: int32 [64, 2], P('seq'), may hold values from 0 to 63, as said below
Outputs:
- d_resid: bfloat16 [8192, 2048], P('seq', 'et')
- d_queries: bfloat16 [8192, 2048], P('seq', 'et')
- d_keys: bfloat16 [8192, 2048], P('seq', 'et')
- d_values: bfloat16 [8192, 2048], P('seq', 'et')
The draws below stay inside these ranges and needn't reach their ends.
Inputs may be any that keep to these rules, and one draw needn't show every extreme that they name: band_bounds[f] = (lo, hi) with max(f - 4, 0) <= lo <= f <= hi <= min(f + 4, 63); in every draw some frames reach 4 frames on each side. `expert_ids`: in each aligned block of 256 tokens, at most 24 assignments name one expert.
All inputs are finite; a program needn't handle non-finite values.
Results may differ from the reference program's by a relative error of at most 0.0095.
Values may be sent and summed in bfloat16 or wider, within the bound.
A program may use at most 64 MiB of HBM per device.

```python
import math
import jax
import jax.numpy as jnp
import numpy as np
from jax import lax

D = 2048
FF = 5632
HEAD = 128
TOP = 2
REACH = 4
SPATIAL = 128
TOK_DEV = 256
FRAMES = 64
TOKENS = 8192
EXPERTS = 32
CAP = 24
N_SEQ = 32


def shared_keys(key):
    base = jnp.clip(jax.random.normal(jax.random.fold_in(key, 21), (TOKENS, D), jnp.float32), -5.0, 5.0)
    return base


def draw_keys(key, part):
    base = shared_keys(key)
    result = base
    return result.astype(jnp.bfloat16)


def draw_queries(key, part):
    key = jax.random.fold_in(key, 8)
    own = jnp.clip(jax.random.normal(key, (TOKENS, D), jnp.float32), -5.0, 5.0)
    result = own
    return result.astype(jnp.bfloat16)


def draw_band_bounds(key, part):
    key = jax.random.fold_in(key, 5)
    frame_ids = jnp.arange(FRAMES, dtype=jnp.int32)
    below = jax.random.randint(jax.random.fold_in(key, 1), (FRAMES,), 0, REACH + 1, jnp.int32)
    above = jax.random.randint(jax.random.fold_in(key, 2), (FRAMES,), 0, REACH + 1, jnp.int32)
    full = frame_ids % (2 * REACH) == REACH
    below = jnp.where(full, REACH, below)
    above = jnp.where(full, REACH, above)
    lower = jnp.maximum(frame_ids - below, 0)
    upper = jnp.minimum(frame_ids + above, FRAMES - 1)
    return jnp.stack([lower, upper], axis=1).astype(jnp.int32)


def level_of(stream_key, dims, split, least, largest):
    gain, own = 1.0, jax.random.fold_in(stream_key, 6)
    for axis_at, shards_of in split:
        draws = jnp.exp(jax.random.uniform(jax.random.fold_in(own, axis_at), (shards_of,), jnp.float32, least / len(split), largest / len(split)))
        gain = gain * jnp.repeat(draws, dims[axis_at] // shards_of).reshape([-1 if axis == axis_at else 1 for axis in range(len(dims))])
    return gain


def shared_out(stream_key, own, number, rows, count, top, reach, skew):
    sequence = jax.random.permutation(stream_key, count)
    packed, common = shares(count, rows * top, reach, skew, True), shares(count, rows * top, reach, skew, False)
    places = jnp.arange(count)

    def named(sizes, rotation):
        used = int((sizes > 0).sum())
        fixed = max(1, used // 4)
        shifted = fixed + (places - fixed + rotation * (used - fixed)) % max(1, count - fixed)
        return jnp.zeros((count,), jnp.int32).at[sequence[jnp.where(places < fixed, places, shifted)]].set(jnp.asarray(sizes, jnp.int32))

    sizes = jnp.where(number % 4 == 0, named(packed, number // 4), named(common, number - number // 4 - 1))
    mixed = jax.random.permutation(jax.random.fold_in(own, 3), count)
    giver, receiver = mixed[0:count // 2 * 2:2], mixed[1:count // 2 * 2:2]
    room = jnp.minimum(sizes[giver] - 1, reach - sizes[receiver]) // 2
    room = jnp.where((giver == sequence[0]) | (receiver == sequence[0]) | (sizes[receiver] == 0), 0, jnp.maximum(room, 0))
    shifted = jax.random.randint(jax.random.fold_in(own, 4), (count // 2,), 0, 1 << 20) % (room + 1)
    sizes = sizes.at[giver].add(-shifted).at[receiver].add(shifted)
    labels = jnp.searchsorted(jnp.cumsum(sizes), jnp.arange(rows * top), side="right").astype(jnp.int32)
    table = labels.reshape(top, rows).T
    table = table[jax.random.permutation(jax.random.fold_in(own, 1), rows)]
    rotation = jax.random.randint(jax.random.fold_in(own, 2), (rows, 1), 0, top)
    return jnp.take_along_axis(table, (jnp.arange(top)[None, :] + rotation) % top, axis=1)


def shares(count, total, bound, lean, full):
    loads = [(1 << 20) // math.isqrt(rank ** lean) + 1 for rank in range(1, count + 1)]
    largest = bound if full else min(bound, max(-(-total // count), total * loads[0] // sum(loads)))
    least = 1 if total - largest >= count - 1 else 0
    counts, spare = [largest] + [least] * (count - 1), total - largest - least * (count - 1)
    while spare > 0:
        free = [i for i in range(1, count) if counts[i] < largest] or [i for i in range(1, count) if counts[i] < bound]
        whole, left = sum([loads[i] for i in free]), spare
        for i in free:
            more = min(bound - counts[i], max(1, left * loads[i] // whole), spare)
            counts[i] = counts[i] + more
            spare = spare - more
    return np.array(counts)


def gaussian(stream_key, extent, spread, bound, cuts=(), kind=jnp.bfloat16):
    loudness = level_of(stream_key, extent, cuts, -0.22, 0.18) if cuts else 1.0
    array = jax.random.normal(stream_key, extent, jnp.float32) * spread * loudness
    return jnp.minimum(jnp.maximum(array, -bound), bound).astype(kind)


def setup_inputs(seed: int = 0) -> dict:
    seeds = jax.random.split(jax.random.key(seed), 12)
    z_in = gaussian(seeds[0], (TOKENS, D), 1.0, 6.0, ((0, 32), (1, 16)))
    out_grad = gaussian(seeds[1], (TOKENS, D), 1.0, 6.0, ((0, 32), (1, 16)))
    gates = jnp.clip(0.2 + 0.8 * jax.random.uniform(seeds[2], (TOKENS, TOP), jnp.float32) ** level_of(seeds[2], (TOKENS, TOP), ((0, 32),), -0.2, 0.2), 0.2, 1.0)
    expert_ids_keys = jax.random.split(jax.random.fold_in(seeds[3], 1), TOKENS // TOK_DEV)
    expert_ids_turns = jax.random.permutation(jax.random.fold_in(seeds[3], 3), TOKENS // TOK_DEV)
    expert_ids = jax.vmap(lambda own, number: shared_out(jax.random.fold_in(seeds[3], 2), own, number, TOK_DEV, EXPERTS, TOP, CAP, 2))(expert_ids_keys, expert_ids_turns).reshape((TOKENS, TOP))
    w_gate = gaussian(seeds[4], (EXPERTS, D, FF), D ** -0.5, 0.125, ((0, 32), (2, 16)))
    w_up = gaussian(seeds[5], (EXPERTS, D, FF), D ** -0.5, 0.125, ((0, 32), (2, 16)))
    w_down = gaussian(seeds[6], (EXPERTS, FF, D), FF ** -0.5, 0.078125, ((0, 32), (1, 16)))
    queries = draw_queries(jax.random.fold_in(seeds[11], 71), 0)
    keys = draw_keys(jax.random.fold_in(seeds[11], 71), 0)
    values = gaussian(seeds[9], (TOKENS, D), 1.0, 6.0, ((0, 32), (1, 16)))
    band_bounds = draw_band_bounds(jax.random.fold_in(seeds[11], 71), 0)
    return {"z_in": z_in, "out_grad": out_grad, "gates": gates, "expert_ids": expert_ids, "w_gate": w_gate, "w_up": w_up, "w_down": w_down, "queries": queries, "keys": keys, "values": values, "band_bounds": band_bounds}


def band_backward(queries, keys, values, d_resid, band_bounds):
    heads = D // HEAD
    shape4 = (FRAMES, SPATIAL, heads, HEAD)
    q_all = queries.reshape(shape4).astype(jnp.float32)
    widths = ((REACH, REACH), (0, 0), (0, 0), (0, 0))
    k_ext = jnp.pad(keys.reshape(shape4).astype(jnp.float32), widths)
    v_ext = jnp.pad(values.reshape(shape4).astype(jnp.float32), widths)
    do_all = d_resid.reshape(shape4).astype(jnp.float32)
    frame_ids = jnp.arange(FRAMES, dtype=jnp.int32)
    lower = band_bounds[:, 0]
    upper = band_bounds[:, 1]
    scale = 1.0 / (HEAD ** 0.5)
    scores = []
    valids = []
    for offset in range(-REACH, REACH + 1):
        key_frame = frame_ids + offset
        valid = (key_frame >= lower) & (key_frame <= upper)
        near = k_ext[offset + REACH: offset + REACH + FRAMES]
        score = jnp.sum(q_all * near, axis=-1) * scale
        scores.append(jnp.where(valid[:, None, None], score, -1e30))
        valids.append(jnp.broadcast_to(valid[:, None, None], score.shape))
    scores = jnp.stack(scores)
    valids = jnp.stack(valids)
    top_score = jnp.max(scores, axis=0)
    weights = jnp.where(valids, jnp.exp(scores - top_score[None]), 0.0)
    probs = weights / jnp.sum(weights, axis=0)[None]
    dprobs = []
    for idx in range(2 * REACH + 1):
        dprobs.append(jnp.sum(do_all * v_ext[idx: idx + FRAMES], axis=-1))
    dprobs = jnp.stack(dprobs)
    delta = jnp.sum(probs * dprobs, axis=0)
    dscore = probs * (dprobs - delta[None])
    dq_acc = jnp.zeros(shape4, jnp.float32)
    dk_ext = jnp.zeros_like(k_ext)
    dv_ext = jnp.zeros_like(v_ext)
    for idx in range(2 * REACH + 1):
        dq_acc = dq_acc + dscore[idx][..., None] * k_ext[idx: idx + FRAMES] * scale
        dk_ext = dk_ext.at[idx: idx + FRAMES].add(dscore[idx][..., None] * q_all * scale)
        dv_ext = dv_ext.at[idx: idx + FRAMES].add(probs[idx][..., None] * do_all)
    d_queries = dq_acc.reshape(TOKENS, D).astype(jnp.bfloat16)
    d_keys = dk_ext[REACH: REACH + FRAMES].reshape(TOKENS, D).astype(jnp.bfloat16)
    d_values = dv_ext[REACH: REACH + FRAMES].reshape(TOKENS, D).astype(jnp.bfloat16)
    return d_queries, d_keys, d_values


def reference(z_in, out_grad, gates, expert_ids, w_gate, w_up, w_down, queries, keys, values, band_bounds):
    assigned = TOKENS * TOP
    block_ids = expert_ids.reshape(N_SEQ, TOK_DEV * TOP)
    onehot = (block_ids[:, :, None] == jnp.arange(EXPERTS, dtype=jnp.int32)[None, None, :]).astype(jnp.int32)
    before = jnp.cumsum(onehot, axis=1) - onehot
    slot_ids = jnp.sum(before * onehot, axis=2)
    position = jnp.arange(N_SEQ, dtype=jnp.int32)[:, None] * CAP + slot_ids
    row_ids = jnp.arange(assigned, dtype=jnp.int32).reshape(N_SEQ, TOK_DEV * TOP)
    table = jnp.full((EXPERTS, N_SEQ * CAP), assigned, jnp.int32).at[block_ids, position].set(row_ids)
    grad_f32 = out_grad.astype(jnp.float32)
    tok_rep = jnp.repeat(z_in, TOP, axis=0)
    scaled = (gates.reshape(assigned, 1) * jnp.repeat(grad_f32, TOP, axis=0)).astype(jnp.bfloat16)
    pad_x = jnp.concatenate([tok_rep, jnp.zeros((1, D), jnp.bfloat16)], axis=0)
    pad_dy = jnp.concatenate([scaled, jnp.zeros((1, D), jnp.bfloat16)], axis=0)

    def one_expert(operands):
        wg, wu, wd, index = operands
        rows_x = pad_x[index]
        rows_dy = pad_dy[index]
        gate_pre = jnp.dot(rows_x, wg, preferred_element_type=jnp.float32)
        up_pre = jnp.dot(rows_x, wu, preferred_element_type=jnp.float32)
        sig = jax.nn.sigmoid(gate_pre)
        d_act = lax.dot_general(rows_dy, wd, (((1,), (1,)), ((), ())), preferred_element_type=jnp.float32)
        d_up = (d_act * gate_pre * sig).astype(jnp.bfloat16)
        d_gate = (d_act * up_pre * sig * (1.0 + gate_pre * (1.0 - sig))).astype(jnp.bfloat16)
        total = lax.dot_general(d_gate, wg, (((1,), (1,)), ((), ())), preferred_element_type=jnp.float32)
        total = total + lax.dot_general(d_up, wu, (((1,), (1,)), ((), ())), preferred_element_type=jnp.float32)
        return total.astype(jnp.bfloat16)

    results = lax.map(one_expert, (w_gate, w_up, w_down, table))
    gathered = jnp.zeros((assigned + 1, D), jnp.float32).at[table.reshape(-1)].add(results.reshape(-1, D).astype(jnp.float32))
    d_stream = grad_f32 + jnp.sum(gathered[:assigned].reshape(TOKENS, TOP, D), axis=1)
    d_resid = d_stream.astype(jnp.bfloat16)
    d_queries, d_keys, d_values = band_backward(queries, keys, values, d_resid, band_bounds)
    return d_resid, d_queries, d_keys, d_values
```

```python
import functools

import jax
import jax.numpy as jnp
from jax import lax
from jax.experimental import pallas as pl
from jax.experimental.pallas import tpu as pltpu
from jax.sharding import PartitionSpec as P

HEAD = 128
REACH = 4
CAP = 24
MSG = 48
BACK = 32
CHUNKS = 4
GROUPS = 2
MESH = pl.DeviceIdType.MESH
F32 = jnp.float32
BF16 = jnp.bfloat16


def nt(a, b):
    return lax.dot_general(a, b, (((1,), (1,)), ((), ())), preferred_element_type=F32)


def nn(a, b):
    return jnp.dot(a, b, preferred_element_type=F32)


def kernel(
    ns, nz,
    z_ref, og_ref, gates_ref, ids_ref, wg_ref, wu_ref, wd_ref, q_ref, k_ref, v_ref, band_ref,
    resid_ref, dq_ref, dk_ref, dv_ref,
    send_buf, rows, w2, wdn, gu, da, dmat, oother, osib, oown,
    rs_out_r, rs_out_l, rs_in_r, rs_in_l, back_buf, back_in, unplace, cols,
    kv, probs, dkv, dkv_out, dkv_in,
    w_sem, a2a_send, a2a_recv, ag_send_r, ag_send_l, ag_recv, sib_send, sib_recv,
    osib_send, osib_recv, rs_send_r, rs_send_l, rs_recv_r, rs_recv_l, back_send, back_recv,
    kv_send, kv_recv, dkv_send, dkv_recv,
):
    me = lax.axis_index("seq")
    et = lax.axis_index("et")
    core = lax.rem(et, 2)
    chip = et // 2
    sibling = et + 1 - 2 * core
    right = lax.rem(chip + 1, nz) * 2 + core
    left = lax.rem(chip + nz - 1, nz) * 2 + core
    tok = z_ref.shape[0]
    ffl = wg_ref.shape[0]
    ffp = wdn.shape[0]
    cs = ns // CHUNKS
    gs = ns // GROUPS
    arow = gs * 16
    brow = gs * 8
    grow = arow + brow
    srow = grow // 2
    half = nz * HEAD
    steps = nz // 2
    pend = []

    def remote(src, dst, ssem, rsem, seq, e):
        return pltpu.make_async_remote_copy(
            src_ref=src, dst_ref=dst, send_sem=ssem, recv_sem=rsem,
            device_id=(seq, e), device_id_type=MESH,
        )

    def go(copy):
        copy.start()
        pend.append(copy)

    barrier = pltpu.get_barrier_semaphore()

    def greet(i, carry):
        pl.semaphore_signal(
            barrier, inc=1, device_id=(lax.rem(me + i, ns), et), device_id_type=MESH
        )
        return carry

    for e in (left, right, sibling):
        pl.semaphore_signal(barrier, inc=1, device_id=(me, e), device_id_type=MESH)
    lax.fori_loop(1, ns, greet, 0)

    def weight_copies(pos):
        par, rel = pos // nz, lax.rem(pos, nz)
        block = lax.rem(chip + rel, nz) * 2 + lax.rem(core + par, 2)
        src = pl.ds(pl.multiple_of(block * HEAD, HEAD), HEAD)
        dst = pl.ds(pl.multiple_of(pos * HEAD, HEAD), HEAD)
        return (
            pltpu.make_async_copy(wg_ref.at[:, src], w2.at[0:ffl, dst], w_sem.at[0, pos]),
            pltpu.make_async_copy(wu_ref.at[:, src], w2.at[ffp : ffp + ffl, dst], w_sem.at[1, pos]),
            pltpu.make_async_copy(wd_ref.at[:, src], wdn.at[0:ffl, dst], w_sem.at[2, pos]),
        )

    def weight_start(pos, carry):
        for copy in weight_copies(pos):
            copy.start()
        return carry

    def weight_wait(pos, carry):
        for copy in weight_copies(pos):
            copy.wait()
        return carry

    lax.fori_loop(0, 2 * nz, weight_start, 0)
    if ffp > ffl:
        pad = jnp.zeros((ffp - ffl, w2.shape[1]), BF16)
        w2[ffl:ffp, :] = pad
        w2[ffp + ffl : 2 * ffp, :] = pad
        wdn[ffl:ffp, :] = pad

    ids = (ids_ref[0:1, :], ids_ref[1:2, :])
    rel = [jnp.bitwise_and(me - i, ns - 1) for i in ids]
    kio = lax.broadcasted_iota(jnp.int32, (ns, tok), 0)
    hot = [(r == kio).astype(F32) for r in rel]
    tri = (
        lax.broadcasted_iota(jnp.int32, (tok, tok), 0)
        < lax.broadcasted_iota(jnp.int32, (tok, tok), 1)
    ).astype(F32).astype(BF16)
    before = nn((hot[0] + hot[1]).astype(BF16), tri)
    slot = [jnp.sum(before * h, axis=0, keepdims=True).astype(jnp.int32) for h in hot]
    rio = lax.broadcasted_iota(jnp.int32, (128, tok), 0)
    packed = jnp.zeros((128, tok), F32)
    for j in range(2):
        target = rel[j] * BACK + slot[j] + jnp.where(
            slot[j] >= 16, 8 * jnp.bitwise_and(rel[j], 1), 0
        )
        packed = jnp.where(rio == j, target.astype(F32), packed)
        packed = jnp.where(rio == 2 + j, gates_ref[j : j + 1, :], packed)
    packed = jnp.transpose(packed)
    cols[...] = packed
    og32 = og_ref[...].astype(F32)
    scaled = [(packed[:, 2 + j : 3 + j] * og32).astype(BF16) for j in range(2)]
    msg_io = lax.broadcasted_iota(jnp.int32, (ns * MSG, tok), 0)
    row_x = [rel[j] * MSG + slot[j] + jnp.where(slot[j] >= 16, 16, 0) for j in range(2)]
    row_d = [rel[j] * MSG + slot[j] + jnp.where(slot[j] >= 16, 24, 16) for j in range(2)]
    hit = ((msg_io == row_x[0]).astype(F32) + (msg_io == row_x[1]).astype(F32)).astype(BF16)
    msgs = nn(hit, z_ref[...])
    for j in range(2):
        msgs = msgs + nn((msg_io == row_d[j]).astype(F32).astype(BF16), scaled[j])
    send_buf[...] = msgs.astype(BF16).reshape(ns, MSG, HEAD)

    frames, spatial = kv.shape[0] - 2 * REACH, kv.shape[2]
    kv[REACH : REACH + frames, 0] = k_ref[...].reshape(frames, spatial, HEAD)
    kv[REACH : REACH + frames, 1] = v_ref[...].reshape(frames, spatial, HEAD)

    pl.semaphore_wait(barrier, ns + 2)

    def dispatch(c):
        def one(k, carry):
            remote(
                send_buf.at[k], rows.at[0, k], a2a_send, a2a_recv.at[c],
                lax.rem(me + ns - k, ns), et,
            ).start()
            return carry

        lax.fori_loop(max(1, c * cs), (c + 1) * cs, one, 0)

    dispatch(0)
    dispatch(1)
    rows[0, 0] = send_buf[0]
    hops = (1, -1, 2, -2)
    kv_copies = []
    for n, h in enumerate(hops):
        at = REACH - frames * h
        copy = remote(
            kv.at[REACH : REACH + frames], kv.at[at : at + frames], kv_send.at[n], kv_recv.at[n],
            lax.rem(me + h + ns, ns), et,
        )
        go(copy)
        kv_copies.append(copy)
    dispatch(2)
    dispatch(3)

    def reach_r(c):
        return steps if c % 2 == 0 else steps - 1

    def reach_l(c):
        return nz - 1 - reach_r(c)

    def chunk_of(pos, c):
        return rows.at[pos, c * cs : (c + 1) * cs]

    ag_r, ag_l, sib = {}, {}, {}

    def send_right(c, s):
        src, dst = (nz - (s - 1)) % nz, nz - s
        ag_r[c, s] = remote(
            chunk_of(src, c), chunk_of(dst, c), ag_send_r.at[c, s - 1], ag_recv.at[c, dst], me, right
        )
        go(ag_r[c, s])

    def send_left(c, s):
        ag_l[c, s] = remote(
            chunk_of(s - 1, c), chunk_of(s, c), ag_send_l.at[c, s - 1], ag_recv.at[c, s], me, left
        )
        go(ag_l[c, s])

    def send_sib(c, r):
        sib[c, r] = remote(
            chunk_of(r, c), chunk_of(nz + r, c), sib_send.at[c, r], sib_recv.at[c, r], me, sibling
        )
        go(sib[c, r])

    def ag_init(c):
        first = max(1, c * cs)
        if (c + 1) * cs > first:
            span = slice(first, (c + 1) * cs)
            remote(
                send_buf.at[span], rows.at[0, span], a2a_send, a2a_recv.at[c], me, et
            ).wait_recv()
        if reach_r(c) >= 1:
            send_right(c, 1)
        if reach_l(c) >= 1:
            send_left(c, 1)
        send_sib(c, 0)

    def ag_step(c, s):
        if s <= reach_r(c):
            ag_r[c, s].wait_recv()
            if s < reach_r(c):
                send_right(c, s + 1)
            send_sib(c, nz - s)
        if s <= reach_l(c):
            ag_l[c, s].wait_recv()
            if s < reach_l(c):
                send_left(c, s + 1)
            send_sib(c, s)

    def ag_finish(c):
        for r in range(nz):
            sib[c, r].wait_recv()

    def tile(g, pos, t):
        block = rows[pos, g * gs : (g + 1) * gs, t * 16 : (t + 1) * 16, :]
        return block.reshape(arow, HEAD)

    def lhs(g, t):
        return jnp.concatenate(
            [
                jnp.concatenate([tile(g, pos, t) for pos in range(2 * nz)], axis=1),
                jnp.concatenate([tile(g, pos, 2) for pos in range(2 * nz)], axis=1),
            ],
            axis=0,
        )

    def gate_up(g, n, width):
        gu[:, n * width : (n + 1) * width] = nt(lhs(g, 0), w2[n * width : (n + 1) * width, :])

    def dact(g):
        da[...] = nt(lhs(g, 1), wdn[...])

    def activation(g):
        def mixed(ref, at, width, off):
            block = ref[arow : 2 * arow, at : at + width].reshape(gs, 16, width)
            return block[:, off : off + 8].reshape(brow, width)

        for lo, hi, gate, up, d_act in (
            (0, arow, gu[0:arow, 0:ffp], gu[0:arow, ffp : 2 * ffp], da[0:arow, :]),
            (arow, grow, mixed(gu, 0, ffp, 0), mixed(gu, ffp, ffp, 0), mixed(da, 0, ffp, 8)),
        ):
            sig = jax.nn.sigmoid(gate)
            dsig = d_act * sig
            dmat[lo:hi, 0:ffp] = (dsig * up * (1.0 + gate * (1.0 - sig))).astype(BF16)
            dmat[lo:hi, ffp : 2 * ffp] = (dsig * gate).astype(BF16)

    osib_copies = {}

    def out_other(g, n):
        at = half + n * 2 * HEAD
        part = nn(dmat[...], w2[:, at : at + 2 * HEAD])
        oother[g, 2 * n] = part[:, 0:HEAD].astype(BF16)
        oother[g, 2 * n + 1] = part[:, HEAD : 2 * HEAD].astype(BF16)
        osib_copies[g, n] = remote(
            oother.at[g, 2 * n : 2 * n + 2], osib.at[g, 2 * n : 2 * n + 2],
            osib_send.at[g, n], osib_recv.at[g, n], me, sibling,
        )
        go(osib_copies[g, n])

    def out_own(g, n):
        at = n * 2 * HEAD
        part = nn(dmat[...], w2[:, at : at + 2 * HEAD])
        oown[g, 2 * n] = part[:, 0:HEAD]
        oown[g, 2 * n + 1] = part[:, HEAD : 2 * HEAD]

    def compute_pieces(g):
        width = 2 * ffp // 3
        pieces = [functools.partial(gate_up, g, n, width) for n in range(3)]
        pieces.append(functools.partial(dact, g))
        pieces.append(functools.partial(activation, g))
        pieces += [functools.partial(out_other, g, n) for n in range(nz // 2)]
        pieces += [functools.partial(out_own, g, n) for n in range(nz // 2)]
        return pieces

    rs_r, rs_l = {}, {}

    def term(g, u, r):
        at = slice(u * srow, (u + 1) * srow)
        return oown[g, r, at, :] + osib[g, r, at, :].astype(F32)

    def rs_send(g, u, s, acc_r, acc_l):
        at = slice(u * srow, (u + 1) * srow)
        if s <= reach_r(u):
            rs_out_r[g, s - 1, at, :] = acc_r.astype(BF16)
            rs_r[g, u, s] = remote(
                rs_out_r.at[g, s - 1, at], rs_in_r.at[g, s - 1, at],
                rs_send_r.at[g, u, s - 1], rs_recv_r.at[g, u, s - 1], me, right,
            )
            go(rs_r[g, u, s])
        if s <= reach_l(u):
            rs_out_l[g, s - 1, at, :] = acc_l.astype(BF16)
            rs_l[g, u, s] = remote(
                rs_out_l.at[g, s - 1, at], rs_in_l.at[g, s - 1, at],
                rs_send_l.at[g, u, s - 1], rs_recv_l.at[g, u, s - 1], me, left,
            )
            go(rs_l[g, u, s])

    def rs_start(g, u):
        if u == 0:
            for n in range(nz // 2):
                osib_copies[g, n].wait_recv()
        first_r = term(g, u, reach_r(u)) if reach_r(u) else None
        first_l = term(g, u, nz - reach_l(u)) if reach_l(u) else None
        rs_send(g, u, 1, first_r, first_l)

    def rs_step(g, u, s):
        at = slice(u * srow, (u + 1) * srow)
        acc_r = acc_l = None
        if s < reach_r(u):
            rs_r[g, u, s].wait_recv()
            acc_r = term(g, u, reach_r(u) - s) + rs_in_r[g, s - 1, at, :].astype(F32)
        if s < reach_l(u):
            rs_l[g, u, s].wait_recv()
            acc_l = term(g, u, nz - reach_l(u) + s) + rs_in_l[g, s - 1, at, :].astype(F32)
        rs_send(g, u, s + 1, acc_r, acc_l)

    def rs_total(g, u):
        at = slice(u * srow, (u + 1) * srow)
        total = term(g, u, 0)
        if reach_r(u):
            rs_r[g, u, reach_r(u)].wait_recv()
            total = total + rs_in_r[g, reach_r(u) - 1, at, :].astype(F32)
        if reach_l(u):
            rs_l[g, u, reach_l(u)].wait_recv()
            total = total + rs_in_l[g, reach_l(u) - 1, at, :].astype(F32)
        return total.astype(BF16)

    def give_back(g):
        total = jnp.concatenate([rs_total(g, u) for u in range(2)], axis=0)
        back_buf[g * gs : (g + 1) * gs, 0:16, :] = total[0:arow].reshape(gs, 16, HEAD)
        pairs = total[arow:grow].reshape(gs // 2, 16, HEAD)
        for i in range(gs):
            back_buf[g * gs + i, 16:32, :] = pairs[i // 2]

        def one(k, carry):
            remote(
                back_buf.at[k], back_in.at[k], back_send, back_recv.at[g],
                lax.rem(me + k, ns), et,
            ).start()
            return carry

        lax.fori_loop(max(1, g * gs), (g + 1) * gs, one, 0)
        if g == 0:
            back_in[0] = back_buf[0]

    def back_wait(g):
        span = slice(max(1, g * gs), (g + 1) * gs)
        remote(back_buf.at[span], back_in.at[span], back_send, back_recv.at[g], me, et).wait_recv()

    def rs_pieces(g):
        pieces = [functools.partial(rs_start, g, u) for u in range(2)]
        for s in range(1, steps):
            pieces += [functools.partial(rs_step, g, u, s) for u in range(2)]
        pieces.append(functools.partial(give_back, g))
        return pieces

    scale = 1.0 / HEAD**0.5
    span = 2 * REACH + 1

    def lane_sum(x):
        return jnp.sum(x, axis=-1, keepdims=True)

    def frame(ref, i):
        return ref[i * spatial : (i + 1) * spatial, :].astype(F32)

    def scores(i):
        if i == 0:
            for copy in kv_copies:
                copy.wait_recv()
        lo, hi = band_ref[i, 0], band_ref[i, 1]
        query = frame(q_ref, i)
        out = []
        for o in range(span):
            at = me * frames + i + o - REACH
            bias = jnp.where((at >= lo) & (at <= hi), jnp.float32(0.0), jnp.float32(-1e30))
            out.append(lane_sum(query * kv[i + o, 0].astype(F32)) * scale + bias)
        top = functools.reduce(jnp.maximum, out)
        weights = [jnp.exp(s - top) for s in out]
        total = functools.reduce(jnp.add, weights)
        for o in range(span):
            probs[i, o] = jnp.broadcast_to(weights[o] / total, (spatial, HEAD))

    def make_unplace():
        lane = lax.broadcasted_iota(jnp.int32, (tok, ns * BACK), 1)
        mark = (lane == cols[:, 0:1].astype(jnp.int32)).astype(F32)
        mark = mark + (lane == cols[:, 1:2].astype(jnp.int32)).astype(F32)
        unplace[...] = mark.astype(BF16)

    def weave(first, second):
        for i in range(max(len(first), len(second))):
            if i < len(first):
                first[i]()
            if i < len(second):
                second[i]()

    def ag_pieces(pair):
        return [
            functools.partial(ag_step, c, s) for s in range(1, steps + 1) for c in pair
        ]

    ag_init(0)
    ag_init(1)
    pieces = ag_pieces((0, 1))
    for piece in pieces[: len(pieces) // 2]:
        piece()
    make_unplace()
    ag_init(2)
    ag_init(3)
    for i in range(frames):
        scores(i)
    for piece in pieces[len(pieces) // 2 :]:
        piece()
    lax.fori_loop(0, 2 * nz, weight_wait, 0)
    ag_finish(0)
    ag_finish(1)
    weave(compute_pieces(0), ag_pieces((2, 3)))
    ag_finish(2)
    ag_finish(3)
    weave(compute_pieces(1), rs_pieces(0))
    for piece in rs_pieces(1):
        piece()
    back_wait(0)
    back_wait(1)

    back = back_in[...].reshape(ns * BACK, HEAD)
    resid = (og_ref[...].astype(F32) + nn(unplace[...], back)).astype(BF16)
    resid_ref[...] = resid

    dkv_copies = []
    dkv[...] = jnp.zeros(dkv.shape, F32)
    for i in range(frames):
        query = frame(q_ref, i) * scale
        cot = resid[i * spatial : (i + 1) * spatial].astype(F32)
        dp = [lane_sum(cot * kv[i + o, 1].astype(F32)) for o in range(span)]
        weighted = [probs[i, o] * dp[o] for o in range(span)]
        delta = functools.reduce(jnp.add, weighted)
        dq = jnp.zeros((spatial, HEAD), F32)
        for o in range(span):
            prob = probs[i, o]
            ds = weighted[o] - prob * delta
            dq = dq + ds * kv[i + o, 0].astype(F32)
            dkv[i + o, 0] += ds * query
            dkv[i + o, 1] += prob * cot
        dq_ref[i * spatial : (i + 1) * spatial, :] = (dq * scale).astype(BF16)
    for n, h in enumerate(hops):
        at = REACH + frames * h
        dkv_out[n] = dkv[at : at + frames].astype(BF16)
        copy = remote(
            dkv_out.at[n], dkv_in.at[n], dkv_send.at[n], dkv_recv.at[n],
            lax.rem(me + h + ns, ns), et,
        )
        go(copy)
        dkv_copies.append(copy)

    remote(send_buf.at[1:ns], rows.at[0, 1:ns], a2a_send, a2a_recv.at[0], me, et).wait_send()
    remote(back_buf.at[1:ns], back_in.at[1:ns], back_send, back_recv.at[0], me, et).wait_send()
    for copy in pend:
        copy.wait_send()

    total = dkv[REACH : REACH + frames]
    for n in range(len(hops)):
        dkv_copies[n].wait_recv()
        total = total + dkv_in[n].astype(F32)
    dk_ref[...] = total[:, 0].reshape(tok, HEAD).astype(BF16)
    dv_ref[...] = total[:, 1].reshape(tok, HEAD).astype(BF16)


def shards(
    z_in, out_grad, gates, expert_ids, w_gate, w_up, w_down, queries, keys, values, band_bounds
):
    tok, cols = z_in.shape
    ns = lax.axis_size("seq")
    ne = lax.axis_size("et")
    nz = ne // 2
    ffl = w_gate.shape[2]
    ffp = -(-ffl // 384) * 384
    width = w_gate.shape[1]
    frames = band_bounds.shape[0]
    spatial = tok // frames
    gs = ns // GROUPS
    arow, brow = gs * 16, gs * 8
    grow = arow + brow
    steps = nz // 2
    vmem = pl.BlockSpec(memory_space=pltpu.VMEM)
    hbm = pl.BlockSpec(memory_space=pl.ANY)
    smem = pl.BlockSpec(memory_space=pltpu.SMEM)
    dma = pltpu.SemaphoreType.DMA
    token = jax.ShapeDtypeStruct((tok, cols), BF16)
    return pl.pallas_call(
        functools.partial(kernel, ns, nz),
        out_shape=(token, token, token, token),
        in_specs=[vmem, vmem, vmem, vmem, hbm, hbm, hbm, vmem, vmem, vmem, smem],
        out_specs=(vmem, vmem, vmem, vmem),
        scratch_shapes=[
            pltpu.VMEM((ns, MSG, cols), BF16),
            pltpu.VMEM((2 * nz, ns, MSG, cols), BF16),
            pltpu.VMEM((2 * ffp, width), BF16),
            pltpu.VMEM((ffp, width), BF16),
            pltpu.VMEM((2 * arow, 2 * ffp), F32),
            pltpu.VMEM((2 * arow, ffp), F32),
            pltpu.VMEM((grow, 2 * ffp), BF16),
            pltpu.VMEM((GROUPS, nz, grow, cols), BF16),
            pltpu.VMEM((GROUPS, nz, grow, cols), BF16),
            pltpu.VMEM((GROUPS, nz, grow, cols), F32),
            pltpu.VMEM((GROUPS, steps, grow, cols), BF16),
            pltpu.VMEM((GROUPS, steps, grow, cols), BF16),
            pltpu.VMEM((GROUPS, steps, grow, cols), BF16),
            pltpu.VMEM((GROUPS, steps, grow, cols), BF16),
            pltpu.VMEM((ns, BACK, cols), BF16),
            pltpu.VMEM((ns, BACK, cols), BF16),
            pltpu.VMEM((tok, ns * BACK), BF16),
            pltpu.VMEM((tok, 128), F32),
            pltpu.VMEM((frames + 2 * REACH, 2, spatial, cols), BF16),
            pltpu.VMEM((frames, 2 * REACH + 1, spatial, cols), F32),
            pltpu.VMEM((frames + 2 * REACH, 2, spatial, cols), F32),
            pltpu.VMEM((4, frames, 2, spatial, cols), BF16),
            pltpu.VMEM((4, frames, 2, spatial, cols), BF16),
            dma((3, 2 * nz)),
            dma,
            dma((CHUNKS,)),
            dma((CHUNKS, steps)),
            dma((CHUNKS, steps)),
            dma((CHUNKS, nz)),
            dma((CHUNKS, nz)),
            dma((CHUNKS, nz)),
            dma((GROUPS, steps)),
            dma((GROUPS, steps)),
            dma((GROUPS, 2, steps)),
            dma((GROUPS, 2, steps)),
            dma((GROUPS, 2, steps)),
            dma((GROUPS, 2, steps)),
            dma,
            dma((GROUPS,)),
            dma((4,)),
            dma((4,)),
            dma((4,)),
            dma((4,)),
        ],
        compiler_params=pltpu.CompilerParams(
            collective_id=0, has_side_effects=True, vmem_limit_bytes=56 * 1024 * 1024
        ),
        cost_estimate=pl.CostEstimate(
            flops=10 * 768 * width * ffl, bytes_accessed=6 * width * ffl, transcendentals=0
        ),
    )(
        z_in, out_grad, gates.T, expert_ids.T,
        w_gate[0].T, w_up[0].T, w_down[0],
        queries, keys, values, band_bounds,
    )


def solution(mesh):
    in_specs = (
        P("seq", "et"),
        P("seq", "et"),
        P("seq", None),
        P("seq", None),
        P("seq", None, "et"),
        P("seq", None, "et"),
        P("seq", "et", None),
        P("seq", "et"),
        P("seq", "et"),
        P("seq", "et"),
        P("seq", None),
    )
    out_specs = (P("seq", "et"), P("seq", "et"), P("seq", "et"), P("seq", "et"))
    return jax.shard_map(shards, mesh=mesh, in_specs=in_specs, out_specs=out_specs, check_vma=False)
```

```python
import functools

import jax
import jax.numpy as jnp
from jax import lax
from jax.experimental import pallas as pl
from jax.experimental.pallas import tpu as pltpu
from jax.sharding import PartitionSpec as P

HEAD = 128
REACH = 4
CAP = 24
MSG = 48
BACK = 32
CHUNKS = 4
GROUPS = 2
MESH = pl.DeviceIdType.MESH
F32 = jnp.float32
BF16 = jnp.bfloat16


def nt(a, b):
    return lax.dot_general(a, b, (((1,), (1,)), ((), ())), preferred_element_type=F32)


def nn(a, b):
    return jnp.dot(a, b, preferred_element_type=F32)


def kernel(
    ns, nz,
    z_ref, og_ref, gates_ref, ids_ref, wg_ref, wu_ref, wd_ref, q_ref, k_ref, v_ref, band_ref,
    out_ref,
    send_buf, rows, w2, wdn, gu, da, dmat, oother, osib, oown,
    rs_out_r, rs_out_l, rs_in_r, rs_in_l, back_buf, back_in, unplace, cols,
    kv, probs, packed_p, cot, terms,
    w_sem, a2a_send, a2a_recv, ag_send_r, ag_send_l, ag_recv, sib_send, sib_recv,
    osib_send, osib_recv, rs_send_r, rs_send_l, rs_recv_r, rs_recv_l, back_send, back_recv,
    kv_send, kv_recv, cot_send, cot_recv, term_send, term_recv,
):
    me = lax.axis_index("seq")
    et = lax.axis_index("et")
    core = lax.rem(et, 2)
    chip = et // 2
    sibling = et + 1 - 2 * core
    right = lax.rem(chip + 1, nz) * 2 + core
    left = lax.rem(chip + nz - 1, nz) * 2 + core
    tok = z_ref.shape[0]
    ffl = wg_ref.shape[0]
    ffp = wdn.shape[0]
    cs, gs = ns // CHUNKS, ns // GROUPS
    arow = gs * 16
    brow = gs * 8
    grow = arow + brow
    srow = grow // 2
    half = nz * HEAD
    steps = nz // 2
    pend = []

    def remote(src, dst, ssem, rsem, seq, e):
        return pltpu.make_async_remote_copy(
            src_ref=src, dst_ref=dst, send_sem=ssem, recv_sem=rsem,
            device_id=(seq, e), device_id_type=MESH,
        )

    def go(copy):
        copy.start()
        pend.append(copy)

    barrier = pltpu.get_barrier_semaphore()

    def greet(i, carry):
        pl.semaphore_signal(
            barrier, inc=1, device_id=(lax.rem(me + i, ns), et), device_id_type=MESH
        )
        return carry

    for e in (left, right, sibling):
        pl.semaphore_signal(barrier, inc=1, device_id=(me, e), device_id_type=MESH)
    lax.fori_loop(1, ns, greet, 0)

    def weight_copies(pos):
        par, rel = pos // nz, lax.rem(pos, nz)
        block = lax.rem(chip + rel, nz) * 2 + lax.rem(core + par, 2)
        src = pl.ds(pl.multiple_of(block * HEAD, HEAD), HEAD)
        dst = pl.ds(pl.multiple_of(pos * HEAD, HEAD), HEAD)
        return (
            pltpu.make_async_copy(wg_ref.at[:, src], w2.at[0:ffl, dst], w_sem.at[0, pos]),
            pltpu.make_async_copy(wu_ref.at[:, src], w2.at[ffp : ffp + ffl, dst], w_sem.at[1, pos]),
            pltpu.make_async_copy(wd_ref.at[:, src], wdn.at[0:ffl, dst], w_sem.at[2, pos]),
        )

    def weight_start(pos, carry):
        for copy in weight_copies(pos):
            copy.start()
        return carry

    def weight_wait(pos, carry):
        for copy in weight_copies(pos):
            copy.wait()
        return carry

    lax.fori_loop(0, 2 * nz, weight_start, 0)
    if ffp > ffl:
        pad = jnp.zeros((ffp - ffl, w2.shape[1]), BF16)
        w2[ffl:ffp, :] = pad
        w2[ffp + ffl : 2 * ffp, :] = pad
        wdn[ffl:ffp, :] = pad

    ids = (ids_ref[0:1, :], ids_ref[1:2, :])
    rel = [jnp.bitwise_and(me - i, ns - 1) for i in ids]
    rel = [jnp.where(r <= ns // 2, jnp.maximum(2 * r - 1, 0), 2 * (ns - r)) for r in rel]
    kio = lax.broadcasted_iota(jnp.int32, (ns, tok), 0)
    hot = [(r == kio).astype(F32) for r in rel]
    tri = (
        lax.broadcasted_iota(jnp.int32, (tok, tok), 0)
        < lax.broadcasted_iota(jnp.int32, (tok, tok), 1)
    ).astype(F32).astype(BF16)
    before = nn((hot[0] + hot[1]).astype(BF16), tri)
    slot = [jnp.sum(before * h, axis=0, keepdims=True).astype(jnp.int32) for h in hot]
    rio = lax.broadcasted_iota(jnp.int32, (128, tok), 0)
    packed = jnp.zeros((128, tok), F32)
    for j in range(2):
        target = rel[j] * BACK + slot[j] + jnp.where(
            slot[j] >= 16, 8 * jnp.bitwise_and(rel[j], 1), 0
        )
        packed = jnp.where(rio == j, target.astype(F32), packed)
        packed = jnp.where(rio == 2 + j, gates_ref[j : j + 1, :], packed)
    packed = jnp.transpose(packed)
    cols[...] = packed
    og32 = og_ref[...].astype(F32)
    scaled = [(packed[:, 2 + j : 3 + j] * og32).astype(BF16) for j in range(2)]
    msg_io = lax.broadcasted_iota(jnp.int32, (ns * MSG, tok), 0)
    row_x = [rel[j] * MSG + slot[j] + jnp.where(slot[j] >= 16, 16, 0) for j in range(2)]
    row_d = [rel[j] * MSG + slot[j] + jnp.where(slot[j] >= 16, 24, 16) for j in range(2)]
    hit = ((msg_io == row_x[0]).astype(F32) + (msg_io == row_x[1]).astype(F32)).astype(BF16)
    msgs = nn(hit, z_ref[...])
    for j in range(2):
        msgs = msgs + nn((msg_io == row_d[j]).astype(F32).astype(BF16), scaled[j])
    send_buf[...] = msgs.astype(BF16).reshape(ns, MSG, HEAD)

    frames, spatial = kv.shape[0] - 2 * REACH, kv.shape[2]
    for n, ref in enumerate((k_ref, v_ref, q_ref)):
        kv[REACH : REACH + frames, n] = ref[...].reshape(frames, spatial, HEAD)

    pl.semaphore_wait(barrier, ns + 2)

    def distance(n):
        return (n + 1) // 2 * (1 - 2 * lax.rem(n + 1, 2))

    def dispatch(c):
        def one(k, carry):
            remote(
                send_buf.at[k], rows.at[0, k], a2a_send, a2a_recv.at[c],
                lax.rem(me + ns - distance(k), ns), et,
            ).start()
            return carry

        lax.fori_loop(max(1, c * cs), (c + 1) * cs, one, 0)

    for c in range(CHUNKS):
        dispatch(c)
    rows[0, 0] = send_buf[0]

    seq_right, seq_left = lax.rem(me + 1, ns), lax.rem(me + ns - 1, ns)

    def halo(ref, step, send_sem, recv_sem):
        own = ref.shape[0] // step // 2
        sent = lambda at, to, n, seq: remote(
            ref.at[at * step : (at + 1) * step], ref.at[to * step : (to + 1) * step],
            send_sem.at[n], recv_sem.at[n], seq, et,
        )
        return (
            sent(own, own - 1, 0, seq_right), sent(own, own + 1, 1, seq_left),
            sent(own - 1, own - 2, 2, seq_right), sent(own + 1, own + 2, 3, seq_left),
        )

    kv_halo = halo(kv, frames, kv_send, kv_recv)
    go(kv_halo[0])
    go(kv_halo[1])

    def hand_on(copies, n):
        copies[n].wait_recv()
        go(copies[n + 2])

    def reach_r(c):
        return steps if c % 2 == 0 else steps - 1

    def reach_l(c):
        return nz - 1 - reach_r(c)

    def chunk_of(pos, c):
        return rows.at[pos, c * cs : (c + 1) * cs]

    ag_r, ag_l, sib = {}, {}, {}

    def send_right(c, s):
        src, dst = (nz - (s - 1)) % nz, nz - s
        ag_r[c, s] = remote(
            chunk_of(src, c), chunk_of(dst, c), ag_send_r.at[c, s - 1], ag_recv.at[c, dst], me, right
        )
        go(ag_r[c, s])

    def send_left(c, s):
        ag_l[c, s] = remote(
            chunk_of(s - 1, c), chunk_of(s, c), ag_send_l.at[c, s - 1], ag_recv.at[c, s], me, left
        )
        go(ag_l[c, s])

    def send_sib(c, r):
        sib[c, r] = remote(
            chunk_of(r, c), chunk_of(nz + r, c), sib_send.at[c, r], sib_recv.at[c, r], me, sibling
        )
        go(sib[c, r])

    def ag_init(c):
        first = max(1, c * cs)
        if (c + 1) * cs > first:
            span = slice(first, (c + 1) * cs)
            remote(
                send_buf.at[span], rows.at[0, span], a2a_send, a2a_recv.at[c], me, et
            ).wait_recv()
        if reach_r(c) >= 1:
            send_right(c, 1)
        if reach_l(c) >= 1:
            send_left(c, 1)
        send_sib(c, 0)

    def ag_right(c, s):
        ag_r[c, s].wait_recv()
        if s < reach_r(c):
            send_right(c, s + 1)
        send_sib(c, nz - s)

    def ag_left(c, s):
        ag_l[c, s].wait_recv()
        if s < reach_l(c):
            send_left(c, s + 1)
        send_sib(c, s)

    def tile(c, pos, t):
        block = rows[pos, c * cs : (c + 1) * cs, t * 16 : (t + 1) * 16, :]
        return block.reshape(cs * 16, HEAD)

    def lhs(c, at, t):
        return jnp.concatenate(
            [jnp.concatenate([tile(c, pos, k) for pos in at], axis=1) for k in (t, 2)], axis=0
        )

    def columns(ref, at):
        return jnp.concatenate([ref[:, pos * HEAD : (pos + 1) * HEAD] for pos in at], axis=1)

    def accumulate(c, s):
        near = sorted({s % nz, (nz - s) % nz})
        for r in near:
            sib[c, r].wait_recv()
        at = near + [nz + r for r in near]
        span = slice(2 * c * cs * 16, 2 * (c + 1) * cs * 16)
        part, other = nt(lhs(c, at, 0), columns(w2, at)), nt(lhs(c, at, 1), columns(wdn, at))
        if s == 0:
            gu[span, :], da[span, :] = part, other
        else:
            gu[span, :] += part
            da[span, :] += other

    def activation(g):
        parts = CHUNKS // GROUPS
        full = slice(2 * g * arow, 2 * (g + 1) * arow)

        def rows_of(ref, at, width, off):
            block = ref[full, at : at + width].reshape(parts, 2, cs * 16, width)
            if off is None:
                return block[:, 0].reshape(arow, width)
            block = block[:, 1].reshape(gs, 16, width)
            return block[:, off : off + 8].reshape(brow, width)

        for lo, hi, off_x, off_d in ((0, arow, None, None), (arow, grow, 0, 8)):
            gate, up = rows_of(gu, 0, ffp, off_x), rows_of(gu, ffp, ffp, off_x)
            d_act = rows_of(da, 0, ffp, off_d)
            sig = jax.nn.sigmoid(gate)
            dsig = d_act * sig
            dmat[lo:hi, 0:ffp] = (dsig * up * (1.0 + gate * (1.0 - sig))).astype(BF16)
            dmat[lo:hi, ffp : 2 * ffp] = (dsig * gate).astype(BF16)

    pairs = [(steps - m, (steps + 1 + m) % nz) for m in range(steps)]
    place = {r: 2 * m + n for m, pair in enumerate(pairs) for n, r in enumerate(pair)}
    osib_copies, osib_here = {}, set()

    def product(par, m):
        at = [par * nz + r for r in pairs[m]]
        return nn(dmat[...], columns(w2, at))

    def out_other(g, m):
        part = product(1, m).astype(BF16)
        oother[g, 2 * m] = part[:, 0:HEAD]
        oother[g, 2 * m + 1] = part[:, HEAD : 2 * HEAD]
        osib_copies[g, m] = remote(
            oother.at[g, 2 * m : 2 * m + 2], osib.at[g, 2 * m : 2 * m + 2],
            osib_send.at[g, m], osib_recv.at[g, m], me, sibling,
        )
        go(osib_copies[g, m])

    def out_own(g, m):
        part = product(0, m)
        oown[g, 2 * m] = part[:, 0:HEAD]
        oown[g, 2 * m + 1] = part[:, HEAD : 2 * HEAD]

    rs_r, rs_l = {}, {}

    def term(g, u, r):
        slot_at, at = place[r], slice(u * srow, (u + 1) * srow)
        if (g, slot_at // 2) not in osib_here:
            osib_here.add((g, slot_at // 2))
            osib_copies[g, slot_at // 2].wait_recv()
        return oown[g, slot_at, at, :] + osib[g, slot_at, at, :].astype(F32)

    def rs_send(g, u, s, acc_r, acc_l):
        at = slice(u * srow, (u + 1) * srow)
        if s <= reach_r(u):
            rs_out_r[g, s - 1, at, :] = acc_r.astype(BF16)
            rs_r[g, u, s] = remote(
                rs_out_r.at[g, s - 1, at], rs_in_r.at[g, s - 1, at],
                rs_send_r.at[g, u, s - 1], rs_recv_r.at[g, u, s - 1], me, right,
            )
            go(rs_r[g, u, s])
        if s <= reach_l(u):
            rs_out_l[g, s - 1, at, :] = acc_l.astype(BF16)
            rs_l[g, u, s] = remote(
                rs_out_l.at[g, s - 1, at], rs_in_l.at[g, s - 1, at],
                rs_send_l.at[g, u, s - 1], rs_recv_l.at[g, u, s - 1], me, left,
            )
            go(rs_l[g, u, s])

    def rs_start(g, u):
        first_r = term(g, u, reach_r(u)) if reach_r(u) else None
        first_l = term(g, u, nz - reach_l(u)) if reach_l(u) else None
        rs_send(g, u, 1, first_r, first_l)

    def rs_step(g, u, s):
        at = slice(u * srow, (u + 1) * srow)
        acc_r = acc_l = None
        if s < reach_r(u):
            rs_r[g, u, s].wait_recv()
            acc_r = term(g, u, reach_r(u) - s) + rs_in_r[g, s - 1, at, :].astype(F32)
        if s < reach_l(u):
            rs_l[g, u, s].wait_recv()
            acc_l = term(g, u, nz - reach_l(u) + s) + rs_in_l[g, s - 1, at, :].astype(F32)
        rs_send(g, u, s + 1, acc_r, acc_l)

    def rs_total(g, u):
        at = slice(u * srow, (u + 1) * srow)
        total = term(g, u, 0)
        if reach_r(u):
            rs_r[g, u, reach_r(u)].wait_recv()
            total = total + rs_in_r[g, reach_r(u) - 1, at, :].astype(F32)
        if reach_l(u):
            rs_l[g, u, reach_l(u)].wait_recv()
            total = total + rs_in_l[g, reach_l(u) - 1, at, :].astype(F32)
        return total.astype(BF16)

    def give_back(g):
        total = jnp.concatenate([rs_total(g, u) for u in range(2)], axis=0)
        back_buf[g * gs : (g + 1) * gs, 0:16, :] = total[0:arow].reshape(gs, 16, HEAD)
        shared = total[arow:grow].reshape(gs // 2, 16, HEAD)
        for i in range(gs):
            back_buf[g * gs + i, 16:32, :] = shared[i // 2]

        def one(k, carry):
            remote(
                back_buf.at[k], back_in.at[k], back_send, back_recv.at[g],
                lax.rem(me + ns + distance(k), ns), et,
            ).start()
            return carry

        lax.fori_loop(max(1, g * gs), (g + 1) * gs, one, 0)
        if g == 0:
            back_in[0] = back_buf[0]

    def back_wait(g):
        span = slice(max(1, g * gs), (g + 1) * gs)
        remote(back_buf.at[span], back_in.at[span], back_send, back_recv.at[g], me, et).wait_recv()

    scale = 1.0 / HEAD**0.5
    span = 2 * REACH + 1

    def lane_sum(x):
        return jnp.sum(x, axis=-1, keepdims=True)

    def frame(ref, i):
        return ref[i * spatial : (i + 1) * spatial, :].astype(F32)

    def scores(i):
        if i == 0:
            kv_halo[2].wait_recv()
            kv_halo[3].wait_recv()
        lo, hi = band_ref[i, 0], band_ref[i, 1]
        query = frame(q_ref, i)
        out = []
        for o in range(span):
            at = me * frames + i + o - REACH
            bias = jnp.where((at >= lo) & (at <= hi), jnp.float32(0.0), jnp.float32(-1e30))
            out.append(lane_sum(query * kv[i + o, 0].astype(F32)) * scale + bias)
        top = functools.reduce(jnp.maximum, out)
        weights = [jnp.exp(s - top) for s in out]
        total = functools.reduce(jnp.add, weights)
        lane = lax.broadcasted_iota(jnp.int32, (spatial, HEAD), 1)
        held = jnp.zeros((spatial, HEAD), F32) if i == 0 else packed_p[...]
        for o in range(span):
            prob = jnp.broadcast_to(weights[o] / total, (spatial, HEAD))
            probs[i, o] = prob
            held = jnp.where(lane == (frames + i) * span + o, prob, held)
        packed_p[...] = held

    def make_unplace():
        lane = lax.broadcasted_iota(jnp.int32, (tok, ns * BACK), 1)
        mark = (lane == cols[:, 0:1].astype(jnp.int32)).astype(F32)
        mark = mark + (lane == cols[:, 1:2].astype(jnp.int32)).astype(F32)
        unplace[...] = mark.astype(BF16)

    def ag_tick(c, s):
        if s <= reach_r(c):
            ag_right(c, s)
        if s <= reach_l(c):
            ag_left(c, s)
        accumulate(c, s - 1)

    def outs(make, g, ms):
        for m in ms:
            make(g, m)

    def each(step_of, g, *args):
        for u in range(2):
            step_of(g, u, *args)

    ag_init(0)
    ag_init(1)
    lax.fori_loop(0, 2 * nz, weight_wait, 0)
    for s in range(1, steps):
        ag_tick(0, s)
        ag_tick(1, s)
        if s == 1:
            ag_init(2)
            ag_init(3)
            continue
        ag_tick(2, s - 1)
        ag_tick(3, s - 1)
        if s == 2:
            hand_on(kv_halo, 0)
            hand_on(kv_halo, 1)
            make_unplace()
    if steps < 3:
        hand_on(kv_halo, 0)
        hand_on(kv_halo, 1)
        make_unplace()
    for i in range(frames):
        scores(i)
    first, rest = range(0, min(2, steps)), range(2, steps)
    ag_tick(0, steps)
    ag_tick(1, steps)
    accumulate(0, steps)
    accumulate(1, steps)
    activation(0)
    if steps > 1:
        ag_tick(2, steps - 1)
    outs(out_other, 0, first)
    if steps > 1:
        ag_tick(3, steps - 1)
    outs(out_own, 0, first)
    each(rs_start, 0)
    outs(out_other, 0, rest)
    ag_tick(2, steps)
    outs(out_own, 0, rest)
    ag_tick(3, steps)
    if steps > 1:
        each(rs_step, 0, 1)
    accumulate(2, steps)
    accumulate(3, steps)
    activation(1)
    outs(out_other, 1, first)
    outs(out_own, 1, first)
    each(rs_start, 1)
    if steps > 2:
        each(rs_step, 0, 2)
    outs(out_other, 1, rest)
    outs(out_own, 1, rest)
    for s in range(3, steps):
        each(rs_step, 1, s - 2)
        each(rs_step, 0, s)
    if steps > 2:
        each(rs_step, 1, steps - 2)
    give_back(0)
    if steps > 1:
        each(rs_step, 1, steps - 1)
    give_back(1)

    remote(send_buf.at[1:ns], rows.at[0, 1:ns], a2a_send, a2a_recv.at[0], me, et).wait_send()
    for copy in pend:
        copy.wait_send()
    pend.clear()
    for g in range(GROUPS):
        back_wait(g)

    back = back_in[...].reshape(ns * BACK, HEAD)
    resid = (og_ref[...].astype(F32) + nn(unplace[...], back)).astype(BF16)
    cot[REACH : REACH + frames] = resid.reshape(frames, spatial, HEAD)
    cot_halo = halo(cot, frames, cot_send, cot_recv)
    go(cot_halo[0])
    go(cot_halo[1])
    out_ref[0] = resid

    lane = lax.broadcasted_iota(jnp.int32, (spatial, HEAD), 1)
    held = packed_p[...]
    dk = [jnp.zeros((spatial, HEAD), F32) for _ in range(frames)]
    dv = [jnp.zeros((spatial, HEAD), F32) for _ in range(frames)]
    own_ds = []
    for i in range(frames):
        do = cot[REACH + i].astype(F32)
        dp = [lane_sum(do * kv[i + o, 1].astype(F32)) for o in range(span)]
        weighted = [probs[i, o] * dp[o] for o in range(span)]
        delta = functools.reduce(jnp.add, weighted)
        ds = [weighted[o] - probs[i, o] * delta for o in range(span)]
        for o in range(span):
            held = jnp.where(lane == i * span + o, ds[o], held)
        own_ds.append(ds)
    used = terms.shape[1]
    terms[2] = jnp.transpose(held)[0:used, :]
    term_halo = halo(terms, 1, term_send, term_recv)
    hand_on(cot_halo, 0)
    hand_on(cot_halo, 1)
    go(term_halo[0])
    go(term_halo[1])
    for i in range(frames):
        dq = functools.reduce(
            jnp.add, [own_ds[i][o] * kv[i + o, 0].astype(F32) for o in range(span)]
        )
        out_ref[1, i * spatial : (i + 1) * spatial, :] = (dq * scale).astype(BF16)
        for j in range(frames):
            o = j - i + REACH
            dk[j] = dk[j] + own_ds[i][o] * kv[REACH + i, 2].astype(F32)
            dv[j] = dv[j] + probs[i, o] * cot[REACH + i].astype(F32)
    hand_on(term_halo, 0)
    hand_on(term_halo, 1)

    for n, h in enumerate((-1, 1, -2, 2)):
        if n >= 2:
            cot_halo[n].wait_recv()
            term_halo[n].wait_recv()
        share = jnp.concatenate([terms[2 + h], jnp.zeros((HEAD - used, spatial), F32)], axis=0)
        share = jnp.transpose(share)
        for i in range(frames):
            at = REACH + frames * h + i
            query, do = kv[at, 2].astype(F32), cot[at].astype(F32)
            for j in range(frames):
                o = j - i - frames * h + REACH
                if 0 <= o < span:
                    col = i * span + o
                    dk[j] = dk[j] + share[:, col : col + 1] * query
                    col = (frames + i) * span + o
                    dv[j] = dv[j] + share[:, col : col + 1] * do
    for j in range(frames):
        out_ref[2, j * spatial : (j + 1) * spatial, :] = (dk[j] * scale).astype(BF16)
        out_ref[3, j * spatial : (j + 1) * spatial, :] = dv[j].astype(BF16)
    remote(back_buf.at[1:ns], back_in.at[1:ns], back_send, back_recv.at[0], me, et).wait_send()
    for copy in pend:
        copy.wait_send()


def hand_over(src, *outs):
    for n, out in enumerate(outs):
        out[...] = src[n]


def shards(
    z_in, out_grad, gates, expert_ids, w_gate, w_up, w_down, queries, keys, values, band_bounds
):
    tok, cols = z_in.shape
    ns = lax.axis_size("seq")
    ne = lax.axis_size("et")
    nz = ne // 2
    ffl = w_gate.shape[2]
    ffp = -(-ffl // 384) * 384
    width = w_gate.shape[1]
    frames = band_bounds.shape[0]
    spatial = tok // frames
    gs = ns // GROUPS
    arow, brow = gs * 16, gs * 8
    grow = arow + brow
    steps = nz // 2
    vmem = pl.BlockSpec(memory_space=pltpu.VMEM)
    hbm = pl.BlockSpec(memory_space=pl.ANY)
    smem = pl.BlockSpec(memory_space=pltpu.SMEM)
    dma = pltpu.SemaphoreType.DMA
    token = jax.ShapeDtypeStruct((tok, cols), BF16)
    terms = -(-2 * frames * (2 * REACH + 1) // 8) * 8
    stacked = pl.pallas_call(
        functools.partial(kernel, ns, nz),
        out_shape=jax.ShapeDtypeStruct((4, tok, cols), BF16),
        in_specs=[vmem, vmem, vmem, vmem, hbm, hbm, hbm, vmem, vmem, vmem, smem],
        out_specs=vmem,
        scratch_shapes=[
            pltpu.VMEM((ns, MSG, cols), BF16),
            pltpu.VMEM((2 * nz, ns, MSG, cols), BF16),
            pltpu.VMEM((2 * ffp, width), BF16),
            pltpu.VMEM((ffp, width), BF16),
            pltpu.VMEM((GROUPS * 2 * arow, 2 * ffp), F32),
            pltpu.VMEM((GROUPS * 2 * arow, ffp), F32),
            pltpu.VMEM((grow, 2 * ffp), BF16),
            pltpu.VMEM((GROUPS, nz, grow, cols), BF16),
            pltpu.VMEM((GROUPS, nz, grow, cols), BF16),
            pltpu.VMEM((GROUPS, nz, grow, cols), F32),
            pltpu.VMEM((GROUPS, steps, grow, cols), BF16),
            pltpu.VMEM((GROUPS, steps, grow, cols), BF16),
            pltpu.VMEM((GROUPS, steps, grow, cols), BF16),
            pltpu.VMEM((GROUPS, steps, grow, cols), BF16),
            pltpu.VMEM((ns, BACK, cols), BF16),
            pltpu.VMEM((ns, BACK, cols), BF16),
            pltpu.VMEM((tok, ns * BACK), BF16),
            pltpu.VMEM((tok, 128), F32),
            pltpu.VMEM((frames + 2 * REACH, 3, spatial, cols), BF16),
            pltpu.VMEM((frames, 2 * REACH + 1, spatial, cols), F32),
            pltpu.VMEM((spatial, cols), F32),
            pltpu.VMEM((frames + 2 * REACH, spatial, cols), BF16),
            pltpu.VMEM((5, terms, spatial), F32),
            dma((3, 2 * nz)),
            dma,
            dma((CHUNKS,)),
            dma((CHUNKS, steps)),
            dma((CHUNKS, steps)),
            dma((CHUNKS, nz)),
            dma((CHUNKS, nz)),
            dma((CHUNKS, nz)),
            dma((GROUPS, steps)),
            dma((GROUPS, steps)),
            dma((GROUPS, 2, steps)),
            dma((GROUPS, 2, steps)),
            dma((GROUPS, 2, steps)),
            dma((GROUPS, 2, steps)),
            dma,
            dma((GROUPS,)),
            dma((4,)),
            dma((4,)),
            dma((4,)),
            dma((4,)),
            dma((4,)),
            dma((4,)),
        ],
        compiler_params=pltpu.CompilerParams(
            collective_id=0, has_side_effects=True, vmem_limit_bytes=56 * 1024 * 1024
        ),
        cost_estimate=pl.CostEstimate(
            flops=10 * 768 * width * ffl, bytes_accessed=6 * width * ffl, transcendentals=0
        ),
    )(
        z_in, out_grad, gates.T, expert_ids.T,
        w_gate[0].T, w_up[0].T, w_down[0],
        queries, keys, values, band_bounds,
    )
    return pl.pallas_call(
        hand_over, out_shape=(token,) * 4, in_specs=[vmem], out_specs=(vmem,) * 4
    )(stacked)


def solution(mesh):
    in_specs = (
        P("seq", "et"),
        P("seq", "et"),
        P("seq", None),
        P("seq", None),
        P("seq", None, "et"),
        P("seq", None, "et"),
        P("seq", "et", None),
        P("seq", "et"),
        P("seq", "et"),
        P("seq", "et"),
        P("seq", None),
    )
    out_specs = (P("seq", "et"), P("seq", "et"), P("seq", "et"), P("seq", "et"))
    return jax.shard_map(shards, mesh=mesh, in_specs=in_specs, out_specs=out_specs, check_vma=False)
```

```python
import functools

import jax
import jax.numpy as jnp
from jax import lax
from jax.experimental import pallas as pl
from jax.experimental.pallas import tpu as pltpu
from jax.sharding import PartitionSpec as P

HEAD = 128
REACH = 4
CAP = 24
MSG = 48
BACK = 32
CHUNKS = 4
GROUPS = 2
PLAN = (
    "D0", "D1", "I0", "D2", "I1", "D3", "W", "T01", "T11", "I2", "T02", "T12", "I3", "T21", "U", "K",
    "T03", "T31", "T13", "T22", "H", "T32", "T04", "T14", "A0", "A1", "T23", "C0", "P0", "T33", "Q0", "S0",
    "p0", "q0", "X0", "X1", "T24", "T34", "A2", "A3", "C1", "P1", "R01", "Q1", "S1", "R02", "p1", "q1",
    "R11", "R03", "R12", "B0", "R13", "B1",
)
MESH = pl.DeviceIdType.MESH
F32 = jnp.float32
BF16 = jnp.bfloat16


def nt(a, b):
    return lax.dot_general(a, b, (((1,), (1,)), ((), ())), preferred_element_type=F32)


def nn(a, b):
    return jnp.dot(a, b, preferred_element_type=F32)


def kernel(
    ns, nz,
    z_hbm, og_hbm, gates_hbm, ids_hbm, wg_ref, wu_ref, wd_ref, q_hbm, k_hbm, v_hbm, band_hbm,
    out_ref,
    z_ref, og_ref, gates_ref, ids_ref, band_ref,
    send_buf, rows, w2, wdn, gu, da, dmat, oother, osib, oown,
    rs_out_r, rs_out_l, rs_in_r, rs_in_l, back_buf, back_in, unplace, cols,
    kv, probs, packed_p, cot, terms,
    in_sem, w_sem, a2a_send, a2a_recv, ag_send_r, ag_send_l, ag_recv, sib_send, sib_recv,
    osib_send, osib_recv, rs_send_r, rs_send_l, rs_recv_r, rs_recv_l, back_send, back_recv,
    kv_send, kv_recv, cot_send, cot_recv, term_send, term_recv,
):
    me = lax.axis_index("seq")
    et = lax.axis_index("et")
    core = lax.rem(et, 2)
    chip = et // 2
    sibling = et + 1 - 2 * core
    right = lax.rem(chip + 1, nz) * 2 + core
    left = lax.rem(chip + nz - 1, nz) * 2 + core
    tok = z_ref.shape[0]
    frames, spatial = kv.shape[0] - 2 * REACH, kv.shape[2]
    ffl = wg_ref.shape[0]
    ffp = wdn.shape[0]
    cs, gs = ns // CHUNKS, ns // GROUPS
    arow = gs * 16
    brow = gs * 8
    grow = arow + brow
    srow = grow // 2
    half = nz * HEAD
    steps = nz // 2
    pend = []

    def remote(src, dst, ssem, rsem, seq, e):
        return pltpu.make_async_remote_copy(
            src_ref=src, dst_ref=dst, send_sem=ssem, recv_sem=rsem,
            device_id=(seq, e), device_id_type=MESH,
        )

    def go(copy):
        copy.start()
        pend.append(copy)

    barrier = pltpu.get_barrier_semaphore()

    def greet(i, carry):
        pl.semaphore_signal(
            barrier, inc=1, device_id=(lax.rem(me + i, ns), et), device_id_type=MESH
        )
        return carry

    for e in (left, right, sibling):
        pl.semaphore_signal(barrier, inc=1, device_id=(me, e), device_id_type=MESH)
    lax.fori_loop(1, ns, greet, 0)

    routing_in = [
        pltpu.make_async_copy(src, dst, in_sem.at[n])
        for n, (src, dst) in enumerate(
            ((ids_hbm, ids_ref), (gates_hbm, gates_ref), (z_hbm, z_ref), (og_hbm, og_ref))
        )
    ]
    halo_in = [pltpu.make_async_copy(band_hbm, band_ref, in_sem.at[4])]
    for n, src in enumerate((k_hbm, v_hbm, q_hbm)):
        for i in range(frames):
            halo_in.append(
                pltpu.make_async_copy(
                    src.at[i * spatial : (i + 1) * spatial], kv.at[REACH + i, n],
                    in_sem.at[5 + n * frames + i],
                )
            )
    for copy in routing_in + halo_in:
        copy.start()

    def weight_copies(pos):
        par, rel = pos // nz, lax.rem(pos, nz)
        block = lax.rem(chip + rel, nz) * 2 + lax.rem(core + par, 2)
        src = pl.ds(pl.multiple_of(block * HEAD, HEAD), HEAD)
        dst = pl.ds(pl.multiple_of(pos * HEAD, HEAD), HEAD)
        return (
            pltpu.make_async_copy(wg_ref.at[:, src], w2.at[0:ffl, dst], w_sem.at[0, pos]),
            pltpu.make_async_copy(wu_ref.at[:, src], w2.at[ffp : ffp + ffl, dst], w_sem.at[1, pos]),
            pltpu.make_async_copy(wd_ref.at[:, src], wdn.at[0:ffl, dst], w_sem.at[2, pos]),
        )

    def weight_start(pos, carry):
        for copy in weight_copies(pos):
            copy.start()
        return carry

    def weight_wait(pos, carry):
        for copy in weight_copies(pos):
            copy.wait()
        return carry

    lax.fori_loop(0, 2 * nz, weight_start, 0)
    if ffp > ffl:
        pad = jnp.zeros((ffp - ffl, w2.shape[1]), BF16)
        w2[ffl:ffp, :] = pad
        w2[ffp + ffl : 2 * ffp, :] = pad
        wdn[ffl:ffp, :] = pad

    for copy in routing_in:
        copy.wait()
    ids = (ids_ref[0:1, :], ids_ref[1:2, :])
    rel = [jnp.bitwise_and(me - i, ns - 1) for i in ids]
    rel = [jnp.where(r <= ns // 2, jnp.maximum(2 * r - 1, 0), 2 * (ns - r)) for r in rel]
    rel = [
        jnp.where(r < cs, r, jnp.where(r >= ns - cs, r - (CHUNKS - 2) * cs, r + cs)) for r in rel
    ]
    kio = lax.broadcasted_iota(jnp.int32, (ns, tok), 0)
    hot = [(r == kio).astype(F32) for r in rel]
    tri = (
        lax.broadcasted_iota(jnp.int32, (tok, tok), 0)
        < lax.broadcasted_iota(jnp.int32, (tok, tok), 1)
    ).astype(F32).astype(BF16)
    before = nn((hot[0] + hot[1]).astype(BF16), tri)
    slot = [jnp.sum(before * h, axis=0, keepdims=True).astype(jnp.int32) for h in hot]
    rio = lax.broadcasted_iota(jnp.int32, (128, tok), 0)
    packed = jnp.zeros((128, tok), F32)
    for j in range(2):
        target = rel[j] * BACK + slot[j] + jnp.where(
            slot[j] >= 16, 8 * jnp.bitwise_and(rel[j], 1), 0
        )
        packed = jnp.where(rio == j, target.astype(F32), packed)
        packed = jnp.where(rio == 2 + j, gates_ref[j : j + 1, :], packed)
    packed = jnp.transpose(packed)
    cols[...] = packed
    og32 = og_ref[...].astype(F32)
    scaled = [(packed[:, 2 + j : 3 + j] * og32).astype(BF16) for j in range(2)]
    msg_io = lax.broadcasted_iota(jnp.int32, (ns * MSG, tok), 0)
    row_x = [rel[j] * MSG + slot[j] + jnp.where(slot[j] >= 16, 16, 0) for j in range(2)]
    row_d = [rel[j] * MSG + slot[j] + jnp.where(slot[j] >= 16, 24, 16) for j in range(2)]
    hit = ((msg_io == row_x[0]).astype(F32) + (msg_io == row_x[1]).astype(F32)).astype(BF16)
    msgs = nn(hit, z_ref[...])
    for j in range(2):
        msgs = msgs + nn((msg_io == row_d[j]).astype(F32).astype(BF16), scaled[j])
    send_buf[...] = msgs.astype(BF16).reshape(ns, MSG, HEAD)

    for copy in halo_in:
        copy.wait()
    pl.semaphore_wait(barrier, ns + 2)

    def distance(n):
        n = n + jnp.where(n < cs, 0, jnp.where(n < 2 * cs, (CHUNKS - 2) * cs, -cs))
        return (n + 1) // 2 * (1 - 2 * lax.rem(n + 1, 2))

    def dispatch(c):
        def one(k, carry):
            remote(
                send_buf.at[k], rows.at[0, k], a2a_send, a2a_recv.at[c],
                lax.rem(me + ns - distance(k), ns), et,
            ).start()
            return carry

        lax.fori_loop(max(1, c * cs), (c + 1) * cs, one, 0)

    rows[0, 0] = send_buf[0]

    seq_right, seq_left = lax.rem(me + 1, ns), lax.rem(me + ns - 1, ns)

    def halo(ref, at, size, by, send_sem, recv_sem):
        def moved(start, to, n, seq):
            return remote(
                ref.at[start : start + size], ref.at[to : to + size],
                send_sem.at[n], recv_sem.at[n], seq, et,
            )

        return (
            moved(at, at - by, 0, seq_right), moved(at, at + by, 1, seq_left),
            moved(at - by, at - 2 * by, 2, seq_right), moved(at + by, at + 2 * by, 3, seq_left),
        )

    kv_halo = halo(kv, REACH, frames, frames, kv_send, kv_recv)

    def hand_on(copies, n):
        copies[n].wait_recv()
        go(copies[n + 2])

    def reach_r(c):
        return steps if c % 2 == 0 else steps - 1

    def reach_l(c):
        return nz - 1 - reach_r(c)

    def chunk_of(pos, c):
        return rows.at[pos, c * cs : (c + 1) * cs]

    ag_r, ag_l, sib = {}, {}, {}

    def send_right(c, s):
        src, dst = (nz - (s - 1)) % nz, nz - s
        ag_r[c, s] = remote(
            chunk_of(src, c), chunk_of(dst, c), ag_send_r.at[c, s - 1], ag_recv.at[c, dst], me, right
        )
        go(ag_r[c, s])

    def send_left(c, s):
        ag_l[c, s] = remote(
            chunk_of(s - 1, c), chunk_of(s, c), ag_send_l.at[c, s - 1], ag_recv.at[c, s], me, left
        )
        go(ag_l[c, s])

    def send_sib(c, r):
        sib[c, r] = remote(
            chunk_of(r, c), chunk_of(nz + r, c), sib_send.at[c, r], sib_recv.at[c, r], me, sibling
        )
        go(sib[c, r])

    def ag_init(c):
        first = max(1, c * cs)
        if (c + 1) * cs > first:
            span = slice(first, (c + 1) * cs)
            remote(
                send_buf.at[span], rows.at[0, span], a2a_send, a2a_recv.at[c], me, et
            ).wait_recv()
        if reach_r(c) >= 1:
            send_right(c, 1)
        if reach_l(c) >= 1:
            send_left(c, 1)
        send_sib(c, 0)

    def ag_right(c, s):
        ag_r[c, s].wait_recv()
        if s < reach_r(c):
            send_right(c, s + 1)
        send_sib(c, nz - s)

    def ag_left(c, s):
        ag_l[c, s].wait_recv()
        if s < reach_l(c):
            send_left(c, s + 1)
        send_sib(c, s)

    def tile(c, pos, t):
        block = rows[pos, c * cs : (c + 1) * cs, t * 16 : (t + 1) * 16, :]
        return block.reshape(cs * 16, HEAD)

    def lhs(c, at, t):
        return jnp.concatenate(
            [jnp.concatenate([tile(c, pos, k) for pos in at], axis=1) for k in (t, 2)], axis=0
        )

    def columns(ref, at):
        return jnp.concatenate([ref[:, pos * HEAD : (pos + 1) * HEAD] for pos in at], axis=1)

    def accumulate(c, s):
        near = sorted({s % nz, (nz - s) % nz})
        for r in near:
            sib[c, r].wait_recv()
        at = near + [nz + r for r in near]
        span = slice(2 * c * cs * 16, 2 * (c + 1) * cs * 16)
        part, other = nt(lhs(c, at, 0), columns(w2, at)), nt(lhs(c, at, 1), columns(wdn, at))
        if s == 0:
            gu[span, :], da[span, :] = part, other
        else:
            gu[span, :] += part
            da[span, :] += other

    def activation(g):
        parts = CHUNKS // GROUPS
        full = slice(2 * g * arow, 2 * (g + 1) * arow)

        def rows_of(ref, at, width, off):
            block = ref[full, at : at + width].reshape(parts, 2, cs * 16, width)
            if off is None:
                return block[:, 0].reshape(arow, width)
            block = block[:, 1].reshape(gs, 16, width)
            return block[:, off : off + 8].reshape(brow, width)

        for lo, hi, off_x, off_d in ((0, arow, None, None), (arow, grow, 0, 8)):
            gate, up = rows_of(gu, 0, ffp, off_x), rows_of(gu, ffp, ffp, off_x)
            d_act = rows_of(da, 0, ffp, off_d)
            sig = jax.nn.sigmoid(gate)
            dsig = d_act * sig
            dmat[lo:hi, 0:ffp] = (dsig * up * (1.0 + gate * (1.0 - sig))).astype(BF16)
            dmat[lo:hi, ffp : 2 * ffp] = (dsig * gate).astype(BF16)

    pairs = [(steps - m, (steps + 1 + m) % nz) for m in range(steps)]
    place = {r: 2 * m + n for m, pair in enumerate(pairs) for n, r in enumerate(pair)}
    osib_copies, osib_here = {}, set()

    def product(par, m):
        at = [par * nz + r for r in pairs[m]]
        return nn(dmat[...], columns(w2, at))

    def out_other(g, m):
        part = product(1, m).astype(BF16)
        oother[g, 2 * m] = part[:, 0:HEAD]
        oother[g, 2 * m + 1] = part[:, HEAD : 2 * HEAD]
        osib_copies[g, m] = remote(
            oother.at[g, 2 * m : 2 * m + 2], osib.at[g, 2 * m : 2 * m + 2],
            osib_send.at[g, m], osib_recv.at[g, m], me, sibling,
        )
        go(osib_copies[g, m])

    def out_own(g, m):
        part = product(0, m)
        oown[g, 2 * m] = part[:, 0:HEAD]
        oown[g, 2 * m + 1] = part[:, HEAD : 2 * HEAD]

    rs_r, rs_l = {}, {}

    def term(g, u, r):
        slot_at, at = place[r], slice(u * srow, (u + 1) * srow)
        if (g, slot_at // 2) not in osib_here:
            osib_here.add((g, slot_at // 2))
            osib_copies[g, slot_at // 2].wait_recv()
        return oown[g, slot_at, at, :] + osib[g, slot_at, at, :].astype(F32)

    def rs_send(g, u, s, acc_r, acc_l):
        at = slice(u * srow, (u + 1) * srow)
        if s <= reach_r(u):
            rs_out_r[g, s - 1, at, :] = acc_r.astype(BF16)
            rs_r[g, u, s] = remote(
                rs_out_r.at[g, s - 1, at], rs_in_r.at[g, s - 1, at],
                rs_send_r.at[g, u, s - 1], rs_recv_r.at[g, u, s - 1], me, right,
            )
            go(rs_r[g, u, s])
        if s <= reach_l(u):
            rs_out_l[g, s - 1, at, :] = acc_l.astype(BF16)
            rs_l[g, u, s] = remote(
                rs_out_l.at[g, s - 1, at], rs_in_l.at[g, s - 1, at],
                rs_send_l.at[g, u, s - 1], rs_recv_l.at[g, u, s - 1], me, left,
            )
            go(rs_l[g, u, s])

    def rs_start(g, u):
        first_r = term(g, u, reach_r(u)) if reach_r(u) else None
        first_l = term(g, u, nz - reach_l(u)) if reach_l(u) else None
        rs_send(g, u, 1, first_r, first_l)

    def rs_step(g, u, s):
        at = slice(u * srow, (u + 1) * srow)
        acc_r = acc_l = None
        if s < reach_r(u):
            rs_r[g, u, s].wait_recv()
            acc_r = term(g, u, reach_r(u) - s) + rs_in_r[g, s - 1, at, :].astype(F32)
        if s < reach_l(u):
            rs_l[g, u, s].wait_recv()
            acc_l = term(g, u, nz - reach_l(u) + s) + rs_in_l[g, s - 1, at, :].astype(F32)
        rs_send(g, u, s + 1, acc_r, acc_l)

    def rs_total(g, u):
        at = slice(u * srow, (u + 1) * srow)
        total = term(g, u, 0)
        if reach_r(u):
            rs_r[g, u, reach_r(u)].wait_recv()
            total = total + rs_in_r[g, reach_r(u) - 1, at, :].astype(F32)
        if reach_l(u):
            rs_l[g, u, reach_l(u)].wait_recv()
            total = total + rs_in_l[g, reach_l(u) - 1, at, :].astype(F32)
        return total.astype(BF16)

    def give_back(g):
        total = jnp.concatenate([rs_total(g, u) for u in range(2)], axis=0)
        back_buf[g * gs : (g + 1) * gs, 0:16, :] = total[0:arow].reshape(gs, 16, HEAD)
        shared = total[arow:grow].reshape(gs // 2, 16, HEAD)
        for i in range(gs):
            back_buf[g * gs + i, 16:32, :] = shared[i // 2]

        def one(k, carry):
            remote(
                back_buf.at[k], back_in.at[k], back_send, back_recv.at[g],
                lax.rem(me + ns + distance(k), ns), et,
            ).start()
            return carry

        lax.fori_loop(max(1, g * gs), (g + 1) * gs, one, 0)
        if g == 0:
            back_in[0] = back_buf[0]

    def back_wait(g):
        span = slice(max(1, g * gs), (g + 1) * gs)
        remote(back_buf.at[span], back_in.at[span], back_send, back_recv.at[g], me, et).wait_recv()

    scale = 1.0 / HEAD**0.5
    span = 2 * REACH + 1

    def lane_sum(x):
        return jnp.sum(x, axis=-1, keepdims=True)

    def scores(i):
        if i == 0:
            kv_halo[2].wait_recv()
            kv_halo[3].wait_recv()
        lo, hi = band_ref[i, 0], band_ref[i, 1]
        query = kv[REACH + i, 2].astype(F32)
        out = []
        for o in range(span):
            at = me * frames + i + o - REACH
            bias = jnp.where((at >= lo) & (at <= hi), jnp.float32(0.0), jnp.float32(-1e30))
            out.append(lane_sum(query * kv[i + o, 0].astype(F32)) * scale + bias)
        top = functools.reduce(jnp.maximum, out)
        weights = [jnp.exp(s - top) for s in out]
        total = functools.reduce(jnp.add, weights)
        lane = lax.broadcasted_iota(jnp.int32, (spatial, HEAD), 1)
        held = jnp.zeros((spatial, HEAD), F32) if i == 0 else packed_p[...]
        for o in range(span):
            prob = jnp.broadcast_to(weights[o] / total, (spatial, HEAD))
            probs[i, o] = prob
            held = jnp.where(lane == (frames + i) * span + o, prob, held)
        packed_p[...] = held

    def make_unplace():
        lane = lax.broadcasted_iota(jnp.int32, (tok, ns * BACK), 1)
        mark = (lane == cols[:, 0:1].astype(jnp.int32)).astype(F32)
        mark = mark + (lane == cols[:, 1:2].astype(jnp.int32)).astype(F32)
        unplace[...] = mark.astype(BF16)

    def ag_tick(c, s):
        if s <= reach_r(c):
            ag_right(c, s)
        if s <= reach_l(c):
            ag_left(c, s)
        accumulate(c, s - 1)

    def kv_out():
        go(kv_halo[0])
        go(kv_halo[1])

    def kv_on():
        hand_on(kv_halo, 0)
        hand_on(kv_halo, 1)

    def weights_here():
        lax.fori_loop(0, 2 * nz, weight_wait, 0)

    def both(step_of, g, *args):
        for u in range(2):
            step_of(g, u, *args)

    def some(make, g, ms):
        for m in ms:
            make(g, m)

    first, rest = range(0, min(2, steps)), range(2, steps)
    for name in PLAN:
        kind, args = name[0], [int(digit) for digit in name[1:]]
        if kind == "T" and args[1] <= steps:
            ag_tick(*args)
        elif kind == "R" and args[1] < steps:
            both(rs_step, *args)
        elif kind == "A":
            accumulate(args[0], steps)
        elif kind in "PpQq":
            make = out_other if kind in "Pp" else out_own
            some(make, args[0], first if kind in "PQ" else rest)
        elif kind == "S":
            both(rs_start, *args)
        elif kind not in "TR":
            step_of = {
                "D": dispatch, "I": ag_init, "W": weights_here, "K": kv_out, "H": kv_on, "U": make_unplace,
                "X": scores, "C": activation, "B": give_back,
            }
            step_of[kind](*args)

    remote(send_buf.at[1:ns], rows.at[0, 1:ns], a2a_send, a2a_recv.at[0], me, et).wait_send()
    for copy in pend:
        copy.wait_send()
    pend.clear()
    for g in range(GROUPS):
        back_wait(g)

    back = back_in[...].reshape(ns * BACK, HEAD)
    cot_halos = []
    for i in range(frames):
        at = slice(i * spatial, (i + 1) * spatial)
        resid = (og_ref[at, :].astype(F32) + nn(unplace[at, :], back)).astype(BF16)
        cot[REACH + i] = resid
        out_ref[0, at, :] = resid
        cot_halos.append(halo(cot, REACH + i, 1, frames, cot_send.at[i], cot_recv.at[i]))
        go(cot_halos[i][0])
        go(cot_halos[i][1])

    lane = lax.broadcasted_iota(jnp.int32, (spatial, HEAD), 1)
    held = packed_p[...]
    dk = [jnp.zeros((spatial, HEAD), F32) for _ in range(frames)]
    dv = [jnp.zeros((spatial, HEAD), F32) for _ in range(frames)]
    own_ds = []
    for i in range(frames):
        do = cot[REACH + i].astype(F32)
        dp = [lane_sum(do * kv[i + o, 1].astype(F32)) for o in range(span)]
        weighted = [probs[i, o] * dp[o] for o in range(span)]
        delta = functools.reduce(jnp.add, weighted)
        ds = [weighted[o] - probs[i, o] * delta for o in range(span)]
        for o in range(span):
            held = jnp.where(lane == i * span + o, ds[o], held)
        own_ds.append(ds)
    used = terms.shape[1]
    terms[2] = jnp.transpose(held)[0:used, :]
    term_halo = halo(terms, 2, 1, 1, term_send, term_recv)
    go(term_halo[0])
    go(term_halo[1])
    for cot_halo in cot_halos:
        hand_on(cot_halo, 0)
        hand_on(cot_halo, 1)
    for i in range(frames):
        dq = functools.reduce(
            jnp.add, [own_ds[i][o] * kv[i + o, 0].astype(F32) for o in range(span)]
        )
        out_ref[1, i * spatial : (i + 1) * spatial, :] = (dq * scale).astype(BF16)
        for j in range(frames):
            o = j - i + REACH
            dk[j] = dk[j] + own_ds[i][o] * kv[REACH + i, 2].astype(F32)
            dv[j] = dv[j] + probs[i, o] * cot[REACH + i].astype(F32)
    hand_on(term_halo, 0)
    hand_on(term_halo, 1)

    for n, h in enumerate((-1, 1, -2, 2)):
        if n >= 2:
            for cot_halo in cot_halos:
                cot_halo[n].wait_recv()
            term_halo[n].wait_recv()
        share = jnp.concatenate([terms[2 + h], jnp.zeros((HEAD - used, spatial), F32)], axis=0)
        share = jnp.transpose(share)
        for i in range(frames):
            at = REACH + frames * h + i
            query, do = kv[at, 2].astype(F32), cot[at].astype(F32)
            for j in range(frames):
                o = j - i - frames * h + REACH
                if 0 <= o < span:
                    col = i * span + o
                    dk[j] = dk[j] + share[:, col : col + 1] * query
                    col = (frames + i) * span + o
                    dv[j] = dv[j] + share[:, col : col + 1] * do
    for j in range(frames):
        out_ref[2, j * spatial : (j + 1) * spatial, :] = (dk[j] * scale).astype(BF16)
        out_ref[3, j * spatial : (j + 1) * spatial, :] = dv[j].astype(BF16)
    remote(back_buf.at[1:ns], back_in.at[1:ns], back_send, back_recv.at[0], me, et).wait_send()
    for copy in pend:
        copy.wait_send()


def hand_over(src, *outs):
    for n, out in enumerate(outs):
        out[...] = src[n]


def shards(
    z_in, out_grad, gates, expert_ids, w_gate, w_up, w_down, queries, keys, values, band_bounds
):
    tok, cols = z_in.shape
    ns = lax.axis_size("seq")
    ne = lax.axis_size("et")
    nz = ne // 2
    ffl = w_gate.shape[2]
    ffp = -(-ffl // 384) * 384
    width = w_gate.shape[1]
    frames = band_bounds.shape[0]
    spatial = tok // frames
    gs = ns // GROUPS
    arow, brow = gs * 16, gs * 8
    grow = arow + brow
    steps = nz // 2
    vmem = pl.BlockSpec(memory_space=pltpu.VMEM)
    hbm = pl.BlockSpec(memory_space=pl.ANY)
    dma = pltpu.SemaphoreType.DMA
    token = jax.ShapeDtypeStruct((tok, cols), BF16)
    terms = -(-2 * frames * (2 * REACH + 1) // 8) * 8
    stacked = pl.pallas_call(
        functools.partial(kernel, ns, nz),
        out_shape=jax.ShapeDtypeStruct((4, tok, cols), BF16),
        in_specs=[hbm] * 11,
        out_specs=vmem,
        scratch_shapes=[
            pltpu.VMEM((tok, cols), BF16),
            pltpu.VMEM((tok, cols), BF16),
            pltpu.VMEM((2, tok), F32),
            pltpu.VMEM((2, tok), jnp.int32),
            pltpu.SMEM((frames, 2), jnp.int32),
            pltpu.VMEM((ns, MSG, cols), BF16),
            pltpu.VMEM((2 * nz, ns, MSG, cols), BF16),
            pltpu.VMEM((2 * ffp, width), BF16),
            pltpu.VMEM((ffp, width), BF16),
            pltpu.VMEM((GROUPS * 2 * arow, 2 * ffp), F32),
            pltpu.VMEM((GROUPS * 2 * arow, ffp), F32),
            pltpu.VMEM((grow, 2 * ffp), BF16),
            pltpu.VMEM((GROUPS, nz, grow, cols), BF16),
            pltpu.VMEM((GROUPS, nz, grow, cols), BF16),
            pltpu.VMEM((GROUPS, nz, grow, cols), F32),
            pltpu.VMEM((GROUPS, steps, grow, cols), BF16),
            pltpu.VMEM((GROUPS, steps, grow, cols), BF16),
            pltpu.VMEM((GROUPS, steps, grow, cols), BF16),
            pltpu.VMEM((GROUPS, steps, grow, cols), BF16),
            pltpu.VMEM((ns, BACK, cols), BF16),
            pltpu.VMEM((ns, BACK, cols), BF16),
            pltpu.VMEM((tok, ns * BACK), BF16),
            pltpu.VMEM((tok, 128), F32),
            pltpu.VMEM((frames + 2 * REACH, 3, spatial, cols), BF16),
            pltpu.VMEM((frames, 2 * REACH + 1, spatial, cols), F32),
            pltpu.VMEM((spatial, cols), F32),
            pltpu.VMEM((frames + 2 * REACH, spatial, cols), BF16),
            pltpu.VMEM((5, terms, spatial), F32),
            dma((5 + 3 * frames,)),
            dma((3, 2 * nz)),
            dma,
            dma((CHUNKS,)),
            dma((CHUNKS, steps)),
            dma((CHUNKS, steps)),
            dma((CHUNKS, nz)),
            dma((CHUNKS, nz)),
            dma((CHUNKS, nz)),
            dma((GROUPS, steps)),
            dma((GROUPS, steps)),
            dma((GROUPS, 2, steps)),
            dma((GROUPS, 2, steps)),
            dma((GROUPS, 2, steps)),
            dma((GROUPS, 2, steps)),
            dma,
            dma((GROUPS,)),
            dma((4,)),
            dma((4,)),
            dma((frames, 4)),
            dma((frames, 4)),
            dma((4,)),
            dma((4,)),
        ],
        compiler_params=pltpu.CompilerParams(
            collective_id=0, has_side_effects=True, vmem_limit_bytes=56 * 1024 * 1024
        ),
        cost_estimate=pl.CostEstimate(
            flops=10 * 768 * width * ffl, bytes_accessed=6 * width * ffl, transcendentals=0
        ),
    )(
        z_in, out_grad, gates.T, expert_ids.T,
        w_gate[0].T, w_up[0].T, w_down[0],
        queries, keys, values, band_bounds,
    )
    return pl.pallas_call(
        hand_over, out_shape=(token,) * 4, in_specs=[vmem], out_specs=(vmem,) * 4
    )(stacked)


def solution(mesh):
    in_specs = (
        P("seq", "et"),
        P("seq", "et"),
        P("seq", None),
        P("seq", None),
        P("seq", None, "et"),
        P("seq", None, "et"),
        P("seq", "et", None),
        P("seq", "et"),
        P("seq", "et"),
        P("seq", "et"),
        P("seq", None),
    )
    out_specs = (P("seq", "et"), P("seq", "et"), P("seq", "et"), P("seq", "et"))
    return jax.shard_map(shards, mesh=mesh, in_specs=in_specs, out_specs=out_specs, check_vma=False)
```

```python
import functools

import jax
import jax.numpy as jnp
from jax import lax
from jax.experimental import pallas as pl
from jax.experimental.pallas import tpu as pltpu
from jax.sharding import PartitionSpec as P

HEAD = 128
REACH = 4
CAP = 24
MSG = 48
BACK = 32
CHUNKS = 4
GROUPS = 2
PLAN = (
    "D0", "D1", "I0", "D2", "I1", "D3", "W", "T01", "T11", "I2", "T02", "T12", "I3", "T21", "U", "K",
    "T03", "T31", "T13", "T22", "H", "T32", "T04", "T14", "A0", "A1", "T23", "C0", "P0", "T33", "Q0", "S0",
    "p0", "q0", "X0", "X1", "T24", "T34", "A2", "A3", "C1", "P1", "R01", "Q1", "S1", "R02", "p1", "q1",
    "R11", "R03", "R12", "B0", "R13", "B1",
)
MESH = pl.DeviceIdType.MESH
F32 = jnp.float32
BF16 = jnp.bfloat16


def nt(a, b):
    return lax.dot_general(a, b, (((1,), (1,)), ((), ())), preferred_element_type=F32)


def nn(a, b):
    return jnp.dot(a, b, preferred_element_type=F32)


def kernel(
    ns, nz,
    z_hbm, og_hbm, gates_hbm, ids_hbm, wg_ref, wu_ref, wd_ref, q_hbm, k_hbm, v_hbm, band_hbm,
    out_ref,
    z_ref, og_ref, gates_ref, ids_ref, band_ref,
    send_buf, rows, w2, wdn, gu, da, dmat, oother, osib, oown,
    rs_out_r, rs_out_l, rs_in_r, rs_in_l, back_buf, back_in, unplace, cols,
    kv, probs, packed_p, cot, terms,
    in_sem, w_sem, a2a_send, a2a_recv, ag_send_r, ag_send_l, ag_recv, sib_send, sib_recv,
    osib_send, osib_recv, rs_send_r, rs_send_l, rs_recv_r, rs_recv_l, back_send, back_recv,
    kv_send, kv_recv, cot_send, cot_recv, term_send, term_recv,
):
    me = lax.axis_index("seq")
    et = lax.axis_index("et")
    core = lax.rem(et, 2)
    chip = et // 2
    sibling = et + 1 - 2 * core
    right = lax.rem(chip + 1, nz) * 2 + core
    left = lax.rem(chip + nz - 1, nz) * 2 + core
    tok = z_ref.shape[0]
    frames, spatial = kv.shape[0] - 2 * REACH, kv.shape[2]
    ffl = wg_ref.shape[0]
    ffp = wdn.shape[0]
    cs, gs = ns // CHUNKS, ns // GROUPS
    arow = gs * 16
    brow = gs * 8
    grow = arow + brow
    srow = grow // 2
    half = nz * HEAD
    steps = nz // 2
    pend = []

    def remote(src, dst, ssem, rsem, seq, e):
        return pltpu.make_async_remote_copy(
            src_ref=src, dst_ref=dst, send_sem=ssem, recv_sem=rsem,
            device_id=(seq, e), device_id_type=MESH,
        )

    def go(copy):
        copy.start()
        pend.append(copy)

    barrier = pltpu.get_barrier_semaphore()

    def greet(i, carry):
        pl.semaphore_signal(
            barrier, inc=1, device_id=(lax.rem(me + i, ns), et), device_id_type=MESH
        )
        return carry

    for e in (left, right, sibling):
        pl.semaphore_signal(barrier, inc=1, device_id=(me, e), device_id_type=MESH)
    lax.fori_loop(1, ns, greet, 0)

    routing_in = [
        pltpu.make_async_copy(src, dst, in_sem.at[n])
        for n, (src, dst) in enumerate(
            ((ids_hbm, ids_ref), (gates_hbm, gates_ref), (z_hbm, z_ref), (og_hbm, og_ref))
        )
    ]
    halo_in = [pltpu.make_async_copy(band_hbm, band_ref, in_sem.at[4])]
    for n, src in enumerate((k_hbm, v_hbm, q_hbm)):
        for i in range(frames):
            halo_in.append(
                pltpu.make_async_copy(
                    src.at[i * spatial : (i + 1) * spatial], kv.at[REACH + i, n],
                    in_sem.at[5 + n * frames + i],
                )
            )
    for copy in routing_in + halo_in:
        copy.start()

    def weight_copies(pos):
        par, rel = pos // nz, lax.rem(pos, nz)
        block = lax.rem(chip + rel, nz) * 2 + lax.rem(core + par, 2)
        src = pl.ds(pl.multiple_of(block * HEAD, HEAD), HEAD)
        dst = pl.ds(pl.multiple_of(pos * HEAD, HEAD), HEAD)
        return (
            pltpu.make_async_copy(wg_ref.at[:, src], w2.at[0:ffl, dst], w_sem.at[0, pos]),
            pltpu.make_async_copy(wu_ref.at[:, src], w2.at[ffp : ffp + ffl, dst], w_sem.at[1, pos]),
            pltpu.make_async_copy(wd_ref.at[:, src], wdn.at[0:ffl, dst], w_sem.at[2, pos]),
        )

    def weight_start(pos, carry):
        for copy in weight_copies(pos):
            copy.start()
        return carry

    def weight_wait(pos, carry):
        for copy in weight_copies(pos):
            copy.wait()
        return carry

    lax.fori_loop(0, 2 * nz, weight_start, 0)
    if ffp > ffl:
        pad = jnp.zeros((ffp - ffl, w2.shape[1]), BF16)
        w2[ffl:ffp, :] = pad
        w2[ffp + ffl : 2 * ffp, :] = pad
        wdn[ffl:ffp, :] = pad

    for copy in routing_in:
        copy.wait()
    ids = (ids_ref[0:1, :], ids_ref[1:2, :])
    rel = [jnp.bitwise_and(me - i, ns - 1) for i in ids]
    rel = [jnp.where(r <= ns // 2, jnp.maximum(2 * r - 1, 0), 2 * (ns - r)) for r in rel]
    rel = [
        jnp.where(r < cs, r, jnp.where(r >= ns - cs, r - (CHUNKS - 2) * cs, r + cs)) for r in rel
    ]
    kio = lax.broadcasted_iota(jnp.int32, (ns, tok), 0)
    hot = [(r == kio).astype(F32) for r in rel]
    tri = (
        lax.broadcasted_iota(jnp.int32, (tok, tok), 0)
        < lax.broadcasted_iota(jnp.int32, (tok, tok), 1)
    ).astype(F32).astype(BF16)
    before = nn((hot[0] + hot[1]).astype(BF16), tri)
    slot = [jnp.sum(before * h, axis=0, keepdims=True).astype(jnp.int32) for h in hot]
    rio = lax.broadcasted_iota(jnp.int32, (128, tok), 0)
    packed = jnp.zeros((128, tok), F32)
    for j in range(2):
        target = rel[j] * BACK + slot[j] + jnp.where(
            slot[j] >= 16, 8 * jnp.bitwise_and(rel[j], 1), 0
        )
        packed = jnp.where(rio == j, target.astype(F32), packed)
        packed = jnp.where(rio == 2 + j, gates_ref[j : j + 1, :], packed)
    packed = jnp.transpose(packed)
    cols[...] = packed
    og32 = og_ref[...].astype(F32)
    scaled = [(packed[:, 2 + j : 3 + j] * og32).astype(BF16) for j in range(2)]
    msg_io = lax.broadcasted_iota(jnp.int32, (ns * MSG, tok), 0)
    row_x = [rel[j] * MSG + slot[j] + jnp.where(slot[j] >= 16, 16, 0) for j in range(2)]
    row_d = [rel[j] * MSG + slot[j] + jnp.where(slot[j] >= 16, 24, 16) for j in range(2)]
    hit = ((msg_io == row_x[0]).astype(F32) + (msg_io == row_x[1]).astype(F32)).astype(BF16)
    msgs = nn(hit, z_ref[...])
    for j in range(2):
        msgs = msgs + nn((msg_io == row_d[j]).astype(F32).astype(BF16), scaled[j])
    send_buf[...] = msgs.astype(BF16).reshape(ns, MSG, HEAD)

    for copy in halo_in:
        copy.wait()
    pl.semaphore_wait(barrier, ns + 2)

    def distance(n):
        n = n + jnp.where(n < cs, 0, jnp.where(n < 2 * cs, (CHUNKS - 2) * cs, -cs))
        return (n + 1) // 2 * (1 - 2 * lax.rem(n + 1, 2))

    def dispatch(c):
        def one(k, carry):
            remote(
                send_buf.at[k], rows.at[0, k], a2a_send, a2a_recv.at[c],
                lax.rem(me + ns - distance(k), ns), et,
            ).start()
            return carry

        lax.fori_loop(max(1, c * cs), (c + 1) * cs, one, 0)

    rows[0, 0] = send_buf[0]

    seq_right, seq_left = lax.rem(me + 1, ns), lax.rem(me + ns - 1, ns)

    def halo(ref, at, size, by, send_sem, recv_sem):
        def moved(start, to, n, seq):
            return remote(
                ref.at[start : start + size], ref.at[to : to + size],
                send_sem.at[n], recv_sem.at[n], seq, et,
            )

        return (
            moved(at, at - by, 0, seq_right), moved(at, at + by, 1, seq_left),
            moved(at - by, at - 2 * by, 2, seq_right), moved(at + by, at + 2 * by, 3, seq_left),
        )

    kv_halo = halo(kv, REACH, frames, frames, kv_send, kv_recv)

    def hand_on(copies, n):
        copies[n].wait_recv()
        go(copies[n + 2])

    def reach_r(c):
        return steps if c % 2 == 0 else steps - 1

    def reach_l(c):
        return nz - 1 - reach_r(c)

    def chunk_of(pos, c):
        return rows.at[pos, c * cs : (c + 1) * cs]

    ag_r, ag_l, sib = {}, {}, {}

    def send_right(c, s):
        src, dst = (nz - (s - 1)) % nz, nz - s
        ag_r[c, s] = remote(
            chunk_of(src, c), chunk_of(dst, c), ag_send_r.at[c, s - 1], ag_recv.at[c, dst], me, right
        )
        go(ag_r[c, s])

    def send_left(c, s):
        ag_l[c, s] = remote(
            chunk_of(s - 1, c), chunk_of(s, c), ag_send_l.at[c, s - 1], ag_recv.at[c, s], me, left
        )
        go(ag_l[c, s])

    def send_sib(c, r):
        sib[c, r] = remote(
            chunk_of(r, c), chunk_of(nz + r, c), sib_send.at[c, r], sib_recv.at[c, r], me, sibling
        )
        go(sib[c, r])

    def ag_init(c):
        first = max(1, c * cs)
        if (c + 1) * cs > first:
            span = slice(first, (c + 1) * cs)
            remote(
                send_buf.at[span], rows.at[0, span], a2a_send, a2a_recv.at[c], me, et
            ).wait_recv()
        if reach_r(c) >= 1:
            send_right(c, 1)
        if reach_l(c) >= 1:
            send_left(c, 1)
        send_sib(c, 0)

    def ag_right(c, s):
        ag_r[c, s].wait_recv()
        if s < reach_r(c):
            send_right(c, s + 1)
        send_sib(c, nz - s)

    def ag_left(c, s):
        ag_l[c, s].wait_recv()
        if s < reach_l(c):
            send_left(c, s + 1)
        send_sib(c, s)

    def tile(c, pos, t):
        block = rows[pos, c * cs : (c + 1) * cs, t * 16 : (t + 1) * 16, :]
        return block.reshape(cs * 16, HEAD)

    def lhs(c, at, t):
        return jnp.concatenate(
            [jnp.concatenate([tile(c, pos, k) for pos in at], axis=1) for k in (t, 2)], axis=0
        )

    def columns(ref, at):
        return jnp.concatenate([ref[:, pos * HEAD : (pos + 1) * HEAD] for pos in at], axis=1)

    def accumulate(c, s):
        near = sorted({s % nz, (nz - s) % nz})
        for r in near:
            sib[c, r].wait_recv()
        at = near + [nz + r for r in near]
        span = slice(2 * c * cs * 16, 2 * (c + 1) * cs * 16)
        part, other = nt(lhs(c, at, 0), columns(w2, at)), nt(lhs(c, at, 1), columns(wdn, at))
        if s == 0:
            gu[span, :], da[span, :] = part, other
        else:
            gu[span, :] += part
            da[span, :] += other

    def activation(g):
        parts = CHUNKS // GROUPS
        full = slice(2 * g * arow, 2 * (g + 1) * arow)

        def rows_of(ref, at, width, off):
            block = ref[full, at : at + width].reshape(parts, 2, cs * 16, width)
            if off is None:
                return block[:, 0].reshape(arow, width)
            block = block[:, 1].reshape(gs, 16, width)
            return block[:, off : off + 8].reshape(brow, width)

        for lo, hi, off_x, off_d in ((0, arow, None, None), (arow, grow, 0, 8)):
            gate, up = rows_of(gu, 0, ffp, off_x), rows_of(gu, ffp, ffp, off_x)
            d_act = rows_of(da, 0, ffp, off_d)
            sig = jax.nn.sigmoid(gate)
            dsig = d_act * sig
            dmat[lo:hi, 0:ffp] = (dsig * up * (1.0 + gate * (1.0 - sig))).astype(BF16)
            dmat[lo:hi, ffp : 2 * ffp] = (dsig * gate).astype(BF16)

    pairs = [(steps - m, (steps + 1 + m) % nz) for m in range(steps)]
    place = {r: 2 * m + n for m, pair in enumerate(pairs) for n, r in enumerate(pair)}
    osib_copies, osib_here = {}, set()

    def product(par, m):
        at = [par * nz + r for r in pairs[m]]
        return nn(dmat[...], columns(w2, at))

    def out_other(g, m):
        part = product(1, m).astype(BF16)
        oother[g, 2 * m] = part[:, 0:HEAD]
        oother[g, 2 * m + 1] = part[:, HEAD : 2 * HEAD]
        osib_copies[g, m] = remote(
            oother.at[g, 2 * m : 2 * m + 2], osib.at[g, 2 * m : 2 * m + 2],
            osib_send.at[g, m], osib_recv.at[g, m], me, sibling,
        )
        go(osib_copies[g, m])

    def out_own(g, m):
        part = product(0, m)
        oown[g, 2 * m] = part[:, 0:HEAD]
        oown[g, 2 * m + 1] = part[:, HEAD : 2 * HEAD]

    rs_r, rs_l = {}, {}

    def term(g, u, r):
        slot_at, at = place[r], slice(u * srow, (u + 1) * srow)
        if (g, slot_at // 2) not in osib_here:
            osib_here.add((g, slot_at // 2))
            osib_copies[g, slot_at // 2].wait_recv()
        return oown[g, slot_at, at, :] + osib[g, slot_at, at, :].astype(F32)

    def rs_send(g, u, s, acc_r, acc_l):
        at = slice(u * srow, (u + 1) * srow)
        if s <= reach_r(u):
            rs_out_r[g, s - 1, at, :] = acc_r.astype(BF16)
            rs_r[g, u, s] = remote(
                rs_out_r.at[g, s - 1, at], rs_in_r.at[g, s - 1, at],
                rs_send_r.at[g, u, s - 1], rs_recv_r.at[g, u, s - 1], me, right,
            )
            go(rs_r[g, u, s])
        if s <= reach_l(u):
            rs_out_l[g, s - 1, at, :] = acc_l.astype(BF16)
            rs_l[g, u, s] = remote(
                rs_out_l.at[g, s - 1, at], rs_in_l.at[g, s - 1, at],
                rs_send_l.at[g, u, s - 1], rs_recv_l.at[g, u, s - 1], me, left,
            )
            go(rs_l[g, u, s])

    def rs_start(g, u):
        first_r = term(g, u, reach_r(u)) if reach_r(u) else None
        first_l = term(g, u, nz - reach_l(u)) if reach_l(u) else None
        rs_send(g, u, 1, first_r, first_l)

    def rs_step(g, u, s):
        at = slice(u * srow, (u + 1) * srow)
        acc_r = acc_l = None
        if s < reach_r(u):
            rs_r[g, u, s].wait_recv()
            acc_r = term(g, u, reach_r(u) - s) + rs_in_r[g, s - 1, at, :].astype(F32)
        if s < reach_l(u):
            rs_l[g, u, s].wait_recv()
            acc_l = term(g, u, nz - reach_l(u) + s) + rs_in_l[g, s - 1, at, :].astype(F32)
        rs_send(g, u, s + 1, acc_r, acc_l)

    def rs_total(g, u):
        at = slice(u * srow, (u + 1) * srow)
        total = term(g, u, 0)
        if reach_r(u):
            rs_r[g, u, reach_r(u)].wait_recv()
            total = total + rs_in_r[g, reach_r(u) - 1, at, :].astype(F32)
        if reach_l(u):
            rs_l[g, u, reach_l(u)].wait_recv()
            total = total + rs_in_l[g, reach_l(u) - 1, at, :].astype(F32)
        return total.astype(BF16)

    def give_back(g):
        total = jnp.concatenate([rs_total(g, u) for u in range(2)], axis=0)
        back_buf[g * gs : (g + 1) * gs, 0:16, :] = total[0:arow].reshape(gs, 16, HEAD)
        shared = total[arow:grow].reshape(gs // 2, 16, HEAD)
        for i in range(gs):
            back_buf[g * gs + i, 16:32, :] = shared[i // 2]

        def one(k, carry):
            remote(
                back_buf.at[k], back_in.at[k], back_send, back_recv.at[g],
                lax.rem(me + ns + distance(k), ns), et,
            ).start()
            return carry

        lax.fori_loop(max(1, g * gs), (g + 1) * gs, one, 0)
        if g == 0:
            back_in[0] = back_buf[0]

    def back_wait(g):
        span = slice(max(1, g * gs), (g + 1) * gs)
        remote(back_buf.at[span], back_in.at[span], back_send, back_recv.at[g], me, et).wait_recv()

    scale = 1.0 / HEAD**0.5
    span = 2 * REACH + 1

    def lane_sum(x):
        return jnp.sum(x, axis=-1, keepdims=True)

    def scores(i):
        if i == 0:
            kv_halo[2].wait_recv()
            kv_halo[3].wait_recv()
        lo, hi = band_ref[i, 0], band_ref[i, 1]
        query = kv[REACH + i, 2].astype(F32)
        out = []
        for o in range(span):
            at = me * frames + i + o - REACH
            bias = jnp.where((at >= lo) & (at <= hi), jnp.float32(0.0), jnp.float32(-1e30))
            out.append(lane_sum(query * kv[i + o, 0].astype(F32)) * scale + bias)
        top = functools.reduce(jnp.maximum, out)
        weights = [jnp.exp(s - top) for s in out]
        total = functools.reduce(jnp.add, weights)
        lane = lax.broadcasted_iota(jnp.int32, (spatial, HEAD), 1)
        held = jnp.zeros((spatial, HEAD), F32) if i == 0 else packed_p[...]
        for o in range(span):
            prob = jnp.broadcast_to(weights[o] / total, (spatial, HEAD))
            probs[i, o] = prob
            held = jnp.where(lane == (frames + i) * span + o, prob, held)
        packed_p[...] = held

    def make_unplace():
        lane = lax.broadcasted_iota(jnp.int32, (tok, ns * BACK), 1)
        mark = (lane == cols[:, 0:1].astype(jnp.int32)).astype(F32)
        mark = mark + (lane == cols[:, 1:2].astype(jnp.int32)).astype(F32)
        unplace[...] = mark.astype(BF16)

    def ag_tick(c, s):
        if s <= reach_r(c):
            ag_right(c, s)
        if s <= reach_l(c):
            ag_left(c, s)
        accumulate(c, s - 1)

    def kv_out():
        go(kv_halo[0])
        go(kv_halo[1])

    def kv_on():
        hand_on(kv_halo, 0)
        hand_on(kv_halo, 1)

    def weights_here():
        lax.fori_loop(0, 2 * nz, weight_wait, 0)

    def both(step_of, g, *args):
        for u in range(2):
            step_of(g, u, *args)

    def some(make, g, ms):
        for m in ms:
            make(g, m)

    first, rest = range(0, min(2, steps)), range(2, steps)
    for name in PLAN:
        kind, args = name[0], [int(digit) for digit in name[1:]]
        if kind == "T" and args[1] <= steps:
            ag_tick(*args)
        elif kind == "R" and args[1] < steps:
            both(rs_step, *args)
        elif kind == "A":
            accumulate(args[0], steps)
        elif kind in "PpQq":
            make = out_other if kind in "Pp" else out_own
            some(make, args[0], first if kind in "PQ" else rest)
        elif kind == "S":
            both(rs_start, *args)
        elif kind not in "TR":
            step_of = {
                "D": dispatch, "I": ag_init, "W": weights_here, "K": kv_out, "H": kv_on, "U": make_unplace,
                "X": scores, "C": activation, "B": give_back,
            }
            step_of[kind](*args)

    remote(send_buf.at[1:ns], rows.at[0, 1:ns], a2a_send, a2a_recv.at[0], me, et).wait_send()
    for copy in pend:
        copy.wait_send()
    pend.clear()
    for g in range(GROUPS):
        back_wait(g)

    back = back_in[...].reshape(ns * BACK, HEAD)
    cot_halos = []
    for i in range(frames):
        at = slice(i * spatial, (i + 1) * spatial)
        resid = (og_ref[at, :].astype(F32) + nn(unplace[at, :], back)).astype(BF16)
        cot[REACH + i] = resid
        out_ref[0, at, :] = resid
        cot_halos.append(halo(cot, REACH + i, 1, frames, cot_send.at[i], cot_recv.at[i]))
        go(cot_halos[i][0])
        go(cot_halos[i][1])

    lane = lax.broadcasted_iota(jnp.int32, (spatial, HEAD), 1)
    held = packed_p[...]
    dk = [jnp.zeros((spatial, HEAD), F32) for _ in range(frames)]
    dv = [jnp.zeros((spatial, HEAD), F32) for _ in range(frames)]
    own_ds = []
    for i in range(frames):
        do = cot[REACH + i].astype(F32)
        dp = [lane_sum(do * kv[i + o, 1].astype(F32)) for o in range(span)]
        weighted = [probs[i, o] * dp[o] for o in range(span)]
        delta = functools.reduce(jnp.add, weighted)
        ds = [weighted[o] - probs[i, o] * delta for o in range(span)]
        for o in range(span):
            held = jnp.where(lane == i * span + o, ds[o], held)
        own_ds.append(ds)
    used = terms.shape[1]
    terms[2] = jnp.transpose(held)[0:used, :]
    term_halo = [
        remote(
            terms.at[2:3], terms.at[2 - h : 3 - h], term_send.at[n], term_recv.at[n],
            lax.rem(me + ns + h, ns), et,
        )
        for n, h in enumerate((1, -1, 2, -2))
    ]
    for copy in term_halo:
        go(copy)
    for cot_halo in cot_halos:
        hand_on(cot_halo, 0)
        hand_on(cot_halo, 1)
    for i in range(frames):
        dq = functools.reduce(
            jnp.add, [own_ds[i][o] * kv[i + o, 0].astype(F32) for o in range(span)]
        )
        out_ref[1, i * spatial : (i + 1) * spatial, :] = (dq * scale).astype(BF16)
        for j in range(frames):
            o = j - i + REACH
            dk[j] = dk[j] + own_ds[i][o] * kv[REACH + i, 2].astype(F32)
            dv[j] = dv[j] + probs[i, o] * cot[REACH + i].astype(F32)

    for n, h in enumerate((-1, 1, -2, 2)):
        if n >= 2:
            for cot_halo in cot_halos:
                cot_halo[n].wait_recv()
        term_halo[n].wait_recv()
        share = jnp.concatenate([terms[2 + h], jnp.zeros((HEAD - used, spatial), F32)], axis=0)
        share = jnp.transpose(share)
        for i in range(frames):
            at = REACH + frames * h + i
            query, do = kv[at, 2].astype(F32), cot[at].astype(F32)
            for j in range(frames):
                o = j - i - frames * h + REACH
                if 0 <= o < span:
                    col = i * span + o
                    dk[j] = dk[j] + share[:, col : col + 1] * query
                    col = (frames + i) * span + o
                    dv[j] = dv[j] + share[:, col : col + 1] * do
    for j in range(frames):
        out_ref[2, j * spatial : (j + 1) * spatial, :] = (dk[j] * scale).astype(BF16)
        out_ref[3, j * spatial : (j + 1) * spatial, :] = dv[j].astype(BF16)
    remote(back_buf.at[1:ns], back_in.at[1:ns], back_send, back_recv.at[0], me, et).wait_send()
    for copy in pend:
        copy.wait_send()


def hand_over(src, *outs):
    for n, out in enumerate(outs):
        out[...] = src[n]


def shards(
    z_in, out_grad, gates, expert_ids, w_gate, w_up, w_down, queries, keys, values, band_bounds
):
    tok, cols = z_in.shape
    ns = lax.axis_size("seq")
    ne = lax.axis_size("et")
    nz = ne // 2
    ffl = w_gate.shape[2]
    ffp = -(-ffl // 384) * 384
    width = w_gate.shape[1]
    frames = band_bounds.shape[0]
    spatial = tok // frames
    gs = ns // GROUPS
    arow, brow = gs * 16, gs * 8
    grow = arow + brow
    steps = nz // 2
    vmem = pl.BlockSpec(memory_space=pltpu.VMEM)
    hbm = pl.BlockSpec(memory_space=pl.ANY)
    dma = pltpu.SemaphoreType.DMA
    token = jax.ShapeDtypeStruct((tok, cols), BF16)
    terms = -(-2 * frames * (2 * REACH + 1) // 8) * 8
    stacked = pl.pallas_call(
        functools.partial(kernel, ns, nz),
        out_shape=jax.ShapeDtypeStruct((4, tok, cols), BF16),
        in_specs=[hbm] * 11,
        out_specs=vmem,
        scratch_shapes=[
            pltpu.VMEM((tok, cols), BF16),
            pltpu.VMEM((tok, cols), BF16),
            pltpu.VMEM((2, tok), F32),
            pltpu.VMEM((2, tok), jnp.int32),
            pltpu.SMEM((frames, 2), jnp.int32),
            pltpu.VMEM((ns, MSG, cols), BF16),
            pltpu.VMEM((2 * nz, ns, MSG, cols), BF16),
            pltpu.VMEM((2 * ffp, width), BF16),
            pltpu.VMEM((ffp, width), BF16),
            pltpu.VMEM((GROUPS * 2 * arow, 2 * ffp), F32),
            pltpu.VMEM((GROUPS * 2 * arow, ffp), F32),
            pltpu.VMEM((grow, 2 * ffp), BF16),
            pltpu.VMEM((GROUPS, nz, grow, cols), BF16),
            pltpu.VMEM((GROUPS, nz, grow, cols), BF16),
            pltpu.VMEM((GROUPS, nz, grow, cols), F32),
            pltpu.VMEM((GROUPS, steps, grow, cols), BF16),
            pltpu.VMEM((GROUPS, steps, grow, cols), BF16),
            pltpu.VMEM((GROUPS, steps, grow, cols), BF16),
            pltpu.VMEM((GROUPS, steps, grow, cols), BF16),
            pltpu.VMEM((ns, BACK, cols), BF16),
            pltpu.VMEM((ns, BACK, cols), BF16),
            pltpu.VMEM((tok, ns * BACK), BF16),
            pltpu.VMEM((tok, 128), F32),
            pltpu.VMEM((frames + 2 * REACH, 3, spatial, cols), BF16),
            pltpu.VMEM((frames, 2 * REACH + 1, spatial, cols), F32),
            pltpu.VMEM((spatial, cols), F32),
            pltpu.VMEM((frames + 2 * REACH, spatial, cols), BF16),
            pltpu.VMEM((5, terms, spatial), F32),
            dma((5 + 3 * frames,)),
            dma((3, 2 * nz)),
            dma,
            dma((CHUNKS,)),
            dma((CHUNKS, steps)),
            dma((CHUNKS, steps)),
            dma((CHUNKS, nz)),
            dma((CHUNKS, nz)),
            dma((CHUNKS, nz)),
            dma((GROUPS, steps)),
            dma((GROUPS, steps)),
            dma((GROUPS, 2, steps)),
            dma((GROUPS, 2, steps)),
            dma((GROUPS, 2, steps)),
            dma((GROUPS, 2, steps)),
            dma,
            dma((GROUPS,)),
            dma((4,)),
            dma((4,)),
            dma((frames, 4)),
            dma((frames, 4)),
            dma((4,)),
            dma((4,)),
        ],
        compiler_params=pltpu.CompilerParams(
            collective_id=0, has_side_effects=True, vmem_limit_bytes=56 * 1024 * 1024
        ),
        cost_estimate=pl.CostEstimate(
            flops=10 * 768 * width * ffl, bytes_accessed=6 * width * ffl, transcendentals=0
        ),
    )(
        z_in, out_grad, gates.T, expert_ids.T,
        w_gate[0].T, w_up[0].T, w_down[0],
        queries, keys, values, band_bounds,
    )
    return pl.pallas_call(
        hand_over, out_shape=(token,) * 4, in_specs=[vmem], out_specs=(vmem,) * 4
    )(stacked)


def solution(mesh):
    in_specs = (
        P("seq", "et"),
        P("seq", "et"),
        P("seq", None),
        P("seq", None),
        P("seq", None, "et"),
        P("seq", None, "et"),
        P("seq", "et", None),
        P("seq", "et"),
        P("seq", "et"),
        P("seq", "et"),
        P("seq", None),
    )
    out_specs = (P("seq", "et"), P("seq", "et"), P("seq", "et"), P("seq", "et"))
    return jax.shard_map(shards, mesh=mesh, in_specs=in_specs, out_specs=out_specs, check_vma=False)
```
